512 devices in a mesh: ctx: 64 (over y, z_hi, core), tp: 8 (over z_lo, x).
Axes of the slice: x: 4, y: 8, z: 8 (z_hi: 4, z_lo: 2; z = z_hi * 2 + z_lo), core: 2. Of those that a mesh axis runs over, the one named last changes fastest.
Arguments:
- queries: bfloat16 [8192, 4096], P('ctx', 'tp'), may hold values from -13.5 to 13.5
- keys: bfloat16 [8192, 1024], P('ctx', 'tp'), may hold values from -4 to 4
- values: bfloat16 [8192, 1024], P('ctx', 'tp'), may hold values from -6 to 6
- saved_out: bfloat16 [8192, 4096], P('ctx', 'tp'), may hold values from -4 to 4
- grad_out: bfloat16 [8192, 4096], P('ctx', 'tp'), may hold values from -48 to 48
- layer_in: bfloat16 [8192, 4096], P('ctx'), may hold values from -6 to 6
Outputs:
- grad_queries: bfloat16 [8192, 4096], P('ctx', 'tp')
- key_gradient: bfloat16 [8192, 1024], P('ctx', 'tp')
- value_gradient: bfloat16 [8192, 1024], P('ctx', 'tp')
- value_weight_direction: bfloat16 [4096, 1024], P('ctx', 'tp')
The draws below stay inside these ranges and needn't reach their ends.
All inputs are finite; a program needn't handle non-finite values.
Results may differ from the reference program's by a relative error of at most 0.0055.
The reference program's roundings to bfloat16 on the way count: a program that leaves them out, or rounds other values in their place, can miss the bound.
Values may be sent and summed in bfloat16 or wider, within the bound.
A program may use at most 64 MiB of HBM per device.

```python
import jax
import jax.numpy as jnp
from jax import lax

MODEL_DIM = 4096
QUERY_HEADS = 32
KEY_VALUE_HEADS = 8
HEAD_SIZE = 128
SHAMPOO_ROWS = 512
NEWTON = 2
SEQUENCE_LENGTH = 8192


def draw_queries(key, part):
    key = jax.random.fold_in(key, 3)
    entry_values = jnp.clip(jax.random.normal(key, (SEQUENCE_LENGTH, QUERY_HEADS * HEAD_SIZE), jnp.float32), -4.0, 4.0)
    return entry_values.astype(jnp.bfloat16)


def draw_keys(key, part):
    key = jax.random.fold_in(key, 5)
    entry_values = jnp.clip(jax.random.normal(key, (SEQUENCE_LENGTH, KEY_VALUE_HEADS * HEAD_SIZE), jnp.float32), -4.0, 4.0)
    return entry_values.astype(jnp.bfloat16)


def level_of(rng, dims, pieces, smallest, top_value):
    def one(axis_at, parts):
        heights = jax.random.uniform(jax.random.fold_in(jax.random.fold_in(rng, 6), axis_at), (parts,), jnp.float32, smallest / len(pieces), top_value / len(pieces))
        return jnp.repeat(jnp.exp(heights), dims[axis_at] // parts).reshape((-1,) + (1,) * (len(dims) - axis_at - 1))

    level = one(*pieces[0])
    for cut in pieces[1:]:
        level = level * one(*cut)
    return level


def scatter_about(stream_key, shape, width, limit, split=(), held_as=jnp.bfloat16):
    array = jax.random.normal(stream_key, shape, jnp.float32) * width
    if len(split) > 0:
        array = level_of(stream_key, shape, split, -0.22, 0.18) * array
    return jnp.clip(array, min=-limit, max=limit).astype(held_as)


def setup_inputs(seed: int = 0) -> dict:
    streams_of = jax.random.split(jax.random.key(seed), 7)
    queries = draw_queries(jax.random.fold_in(streams_of[6], 71), 0)
    keys = draw_keys(jax.random.fold_in(streams_of[6], 71), 0)
    values = scatter_about(streams_of[2], (SEQUENCE_LENGTH, KEY_VALUE_HEADS * HEAD_SIZE), 1.0, 6.0, ((0, 64), (1, 8)))
    saved_out = scatter_about(streams_of[3], (SEQUENCE_LENGTH, QUERY_HEADS * HEAD_SIZE), 0.5, 4.0, ((0, 64), (1, 8)))
    grad_out = scatter_about(streams_of[4], (SEQUENCE_LENGTH, QUERY_HEADS * HEAD_SIZE), 8.0, 48.0, ((0, 64), (1, 8)))
    layer_in = scatter_about(streams_of[5], (SEQUENCE_LENGTH, MODEL_DIM), 1.0, 6.0, ((0, 64),))
    return dict(queries=queries, keys=keys, values=values, saved_out=saved_out, grad_out=grad_out, layer_in=layer_in)


masked_fill = -1e+30
highest = lax.Precision.HIGHEST

def rounded(values_in):
    return lax.optimization_barrier(values_in.astype(jnp.bfloat16)).astype(jnp.float32)

def head_group(operands):
    query_grp, key_one, value_one, saved_grp, cotan_grp = operands
    score_scale = HEAD_SIZE ** (-0.5)
    sequence_length = query_grp.shape[0]
    q_block = min(512, sequence_length)
    query_grads = []
    key_grad = jnp.zeros((sequence_length, HEAD_SIZE), jnp.float32)
    value_grad = jnp.zeros((sequence_length, HEAD_SIZE), jnp.float32)
    for number in range(sequence_length // q_block):
        first_row = number * q_block
        last_row = first_row + q_block
        query_rows = query_grp[first_row:last_row].astype(jnp.float32)
        cotan_rows = cotan_grp[first_row:last_row].astype(jnp.float32)
        saved_rows = saved_grp[first_row:last_row].astype(jnp.float32)
        key_seen = key_one[:last_row].astype(jnp.float32)
        value_seen = value_one[:last_row].astype(jnp.float32)
        scores = jnp.einsum('trd,sd->rts', query_rows, key_seen) * score_scale
        query_pos = first_row + jnp.arange(q_block, dtype=jnp.int32)[:, None]
        key_pos = jnp.arange(last_row, dtype=jnp.int32)[None, :]
        visible = (key_pos <= query_pos)[None]
        masked = jnp.where(visible, scores, masked_fill)
        row_max = lax.optimization_barrier(jnp.max(masked, axis=-1, keepdims=True))
        log_total = row_max + jnp.log(lax.optimization_barrier(jnp.sum(jnp.where(visible, jnp.exp(masked - row_max), 0.0), axis=-1, keepdims=True)))
        probs = jnp.where(visible, jnp.exp(scores - log_total), 0.0)
        row_delta = lax.optimization_barrier(jnp.sum(cotan_rows * saved_rows, axis=-1))
        dprobs = jnp.einsum('trd,sd->rts', cotan_rows, value_seen)
        score_gradient = rounded(probs * (dprobs - row_delta.T[:, :, None]) * score_scale)
        query_grads.append(jnp.einsum('rts,sd->trd', score_gradient, key_seen).astype(jnp.bfloat16))
        key_grad = key_grad.at[:last_row].add(jnp.einsum('rts,trd->sd', score_gradient, query_rows))
        value_grad = value_grad.at[:last_row].add(jnp.einsum('rts,trd->sd', rounded(probs), cotan_rows))
    return (jnp.concatenate(query_grads, 0), key_grad.astype(jnp.bfloat16), value_grad.astype(jnp.bfloat16))

def matmul_high(first_mat, second_mat):
    return jnp.dot(first_mat, second_mat, precision=highest, preferred_element_type=jnp.float32)

def inverse_root(statistic):
    dim_size = statistic.shape[0]
    identity = jnp.eye(dim_size, dtype=jnp.float32)
    matrix = statistic / jnp.sqrt(jnp.sum(statistic * statistic))
    root_est = identity
    for iteration in range(NEWTON):
        factor = (5.0 * identity - matrix) * 0.25
        root_est = matmul_high(root_est, factor)
        square = matmul_high(factor, factor)
        matrix = matmul_high(matmul_high(square, square), matrix)
    return root_est

def shampoo_block(grad_block):
    squares = jnp.sum(grad_block * grad_block)
    left_stat = matmul_high(grad_block, grad_block.T) + (0.1 * squares / SHAMPOO_ROWS + 1e-06) * jnp.eye(SHAMPOO_ROWS, dtype=jnp.float32)
    right_stat = matmul_high(grad_block.T, grad_block) + (0.1 * squares / HEAD_SIZE + 1e-06) * jnp.eye(HEAD_SIZE, dtype=jnp.float32)
    precond = matmul_high(matmul_high(inverse_root(left_stat), grad_block), inverse_root(right_stat))
    return precond / jnp.sqrt(jnp.mean(precond * precond) + 1e-06)

def reference(queries, keys, values, saved_out, grad_out, layer_in):
    heads_per_group = QUERY_HEADS // KEY_VALUE_HEADS
    sequence_length = queries.shape[0]

    def split_heads(sender_index):
        return sender_index.reshape(sequence_length, KEY_VALUE_HEADS, heads_per_group, HEAD_SIZE).transpose(1, 0, 2, 3)
    heads_of_keys = keys.reshape(sequence_length, KEY_VALUE_HEADS, HEAD_SIZE).transpose(1, 0, 2)
    heads_of_values = values.reshape(sequence_length, KEY_VALUE_HEADS, HEAD_SIZE).transpose(1, 0, 2)
    query_out, key_result, value_result = lax.map(head_group, (split_heads(queries), heads_of_keys, heads_of_values, split_heads(saved_out), split_heads(grad_out)))
    grad_queries = query_out.transpose(1, 0, 2, 3).reshape(sequence_length, QUERY_HEADS * HEAD_SIZE)
    key_gradient = key_result.transpose(1, 0, 2).reshape(sequence_length, KEY_VALUE_HEADS * HEAD_SIZE)
    value_gradient = value_result.transpose(1, 0, 2).reshape(sequence_length, KEY_VALUE_HEADS * HEAD_SIZE)
    weight_gradient = jnp.dot(layer_in.T, value_gradient, preferred_element_type=jnp.float32)
    rows_per_block = MODEL_DIM // SHAMPOO_ROWS
    block_list = weight_gradient.reshape(rows_per_block, SHAMPOO_ROWS, KEY_VALUE_HEADS, HEAD_SIZE).transpose(0, 2, 1, 3).reshape(rows_per_block * KEY_VALUE_HEADS, SHAMPOO_ROWS, HEAD_SIZE)
    direction_list = lax.map(shampoo_block, block_list)
    value_weight_direction = direction_list.reshape(rows_per_block, KEY_VALUE_HEADS, SHAMPOO_ROWS, HEAD_SIZE).transpose(0, 2, 1, 3).reshape(MODEL_DIM, KEY_VALUE_HEADS * HEAD_SIZE).astype(jnp.bfloat16)
    return (grad_queries, key_gradient, value_gradient, value_weight_direction)
```

```python
import functools

import jax
import jax.numpy as jnp
from jax import lax
from jax.experimental import pallas as pl
from jax.experimental.pallas import tpu as pltpu
from jax.sharding import PartitionSpec as P

HEAD = 128
Y, Z, CORES = 8, 4, 2
HEADS = 4
ROWS = 256
ALL_ROWS = HEADS * ROWS
CHUNK = Z * 128
NEWTON = 2
BLOCK_ROWS = 512
FILL = -1e30
SCALE = HEAD ** (-0.5)
SCALE2 = SCALE * 1.4426950408889634
HIGHEST = lax.Precision.HIGHEST
F32 = jnp.float32
BF16 = jnp.bfloat16

KZ, VZ, SIB, RK, RV, LSE, SV, SK, ZV, ZK, DQ, WC, WY, WZ, GC, N_SEMS = (
    0, 3, 6, 18, 25, 32, 33, 40, 47, 50, 53, 54, 55, 62, 65, 66,
)


def dot(a, b, dims=(((1,), (0,)), ((), ())), precision=None):
    return lax.dot_general(a, b, dims, precision=precision, preferred_element_type=F32)


def dot_high(a, b):
    return dot(a, b, precision=HIGHEST)


def kernel(
    q_ref, k_ref, v_ref, o_ref, do_ref, x_ref,
    dq_out, dk_out, dv_out, w_out,
    kbuf, vbuf, qs, dos, os, q_t, do_t, delta, m_run, l_run, lse, lse_in, dq_t,
    tmp_v, tmp_k, out_v, out_k, in_v, in_k, zout_v, zout_k, zin_v, zin_k,
    dq_keep, dq_send, dq_in, w_keep, w_send, w_in, wy_out, wy_in, wz_out, wz_in, g_out, g_in, p_scr,
    send, recv,
):
    c = lax.axis_index("ctx")
    core = lax.rem(c, 2)
    z = lax.rem(c // 2, Z)
    y = c // (2 * Z)

    def dev(yy, zz, cc):
        return {"ctx": (yy * Z + zz) * 2 + cc}

    sibling = dev(y, z, 1 - core)

    def at_y(step):
        return lax.rem(y + step + Y, Y)

    def at_z(step):
        return lax.rem(z + step, Z)

    def copy(src, dst, number, device):
        return pltpu.make_async_remote_copy(
            src_ref=src, dst_ref=dst, send_sem=send.at[number], recv_sem=recv.at[number],
            device_id=device, device_id_type=pl.DeviceIdType.MESH,
        )

    barrier = pltpu.get_barrier_semaphore()
    partners = [dev(at_y(i), z, core) for i in range(1, Y)]
    partners += [dev(y, at_z(i), core) for i in range(1, Z)] + [sibling]
    for partner in partners:
        pl.semaphore_signal(barrier, inc=1, device_id=partner, device_id_type=pl.DeviceIdType.MESH)
    pl.semaphore_wait(barrier, len(partners))

    kz = [copy(k_ref, kbuf.at[y, z], KZ + i - 1, dev(y, at_z(i), core)) for i in range(1, Z)]
    vz = [copy(v_ref, vbuf.at[y, z], VZ + i - 1, dev(y, at_z(i), core)) for i in range(1, Z)]
    for one in kz + vz:
        one.start()
    own_rows = [pl.ds(pl.multiple_of(h * ROWS + core * 128, 128), 128) for h in range(HEADS)]
    sib = []
    for n, (ref, buf) in enumerate(((q_ref, qs), (do_ref, dos), (o_ref, os))):
        for h in range(HEADS):
            sib.append(
                copy(ref.at[:, pl.ds(h * HEAD, HEAD)], buf.at[own_rows[h]], SIB + n * HEADS + h, sibling)
            )
    for one in sib:
        one.start()
    for ref, buf in ((q_ref, qs), (do_ref, dos), (o_ref, os)):
        for h in range(HEADS):
            buf[own_rows[h], :] = ref[:, h * HEAD : (h + 1) * HEAD]
    kbuf[y, z] = k_ref[...]
    vbuf[y, z] = v_ref[...]
    m_run[...] = jnp.full(m_run.shape, FILL, F32)
    l_run[...] = jnp.zeros(l_run.shape, F32)
    dq_t[...] = jnp.zeros(dq_t.shape, F32)
    for one in sib:
        one.wait_recv()
    for h in range(HEADS):
        rows = slice(h * ROWS, (h + 1) * ROWS)
        cot = dos[rows, :].astype(F32)
        q_t[:, rows] = qs[rows, :].astype(F32).T.astype(BF16)
        do_t[:, rows] = cot.T.astype(BF16)
        delta[:, rows] = jnp.broadcast_to(
            jnp.sum((cot * os[rows, :].astype(F32)).T, axis=0, keepdims=True), (8, ROWS)
        )

    def scores(keys, h, diagonal):
        s = dot(keys, q_t[:, h * ROWS : (h + 1) * ROWS]) * SCALE2
        if diagonal:
            key = lax.broadcasted_iota(jnp.int32, (CHUNK, ROWS), 0)
            key = key + (key >> 7) * 128 + core * 128
            row = lax.broadcasted_iota(jnp.int32, (CHUNK, ROWS), 1) + z * ROWS
            s = jnp.where(key <= row, s, FILL)
        return s

    def forward(chunk, diagonal):
        keys = kbuf[chunk].reshape(CHUNK, HEAD)
        for h in range(HEADS):
            cols = slice(h * ROWS, (h + 1) * ROWS)
            s = scores(keys, h, diagonal).reshape(CHUNK // 8, 8, ROWS)
            old = m_run[:, cols]
            new = jnp.maximum(old, jnp.max(s, axis=0))
            l_run[:, cols] = l_run[:, cols] * jnp.exp2(old - new) + jnp.sum(jnp.exp2(s - new[None]), axis=0)
            m_run[:, cols] = new

    def ring_copies(t):
        up = lax.rem(t, 2) == 0
        s = t // 2
        chunk = jnp.where(up, at_y(-s), at_y(s))
        target = dev(jnp.where(up, at_y(1), at_y(-1)), z, core)
        return [copy(buf.at[chunk], buf.at[chunk], base + t, target) for buf, base in ((kbuf, RK), (vbuf, RV))]

    def ring_waits(t):
        up = lax.rem(t, 2) == 0
        s = t // 2
        chunk = jnp.where(up, at_y(-1 - s), at_y(1 + s))
        waits = [copy(buf.at[chunk], buf.at[chunk], base + t, sibling) for buf, base in ((kbuf, RK), (vbuf, RV))]
        return chunk, waits

    for one in kz + vz:
        one.wait_recv()

    def gather_step(t, _):
        @pl.when(t >= 2)
        def _():
            _, waits = ring_waits(t - 2)
            for one in waits:
                one.wait_recv()

        for one in ring_copies(t):
            one.start()

        @pl.when(t == 0)
        def _():
            forward(y, True)

        @pl.when(t >= 2)
        def _():
            chunk, _ = ring_waits(t - 2)

            @pl.when(chunk < y)
            def _():
                forward(chunk, False)

        return 0

    lax.fori_loop(0, 7, gather_step, 0)

    def gather_end(t, _):
        chunk, waits = ring_waits(t)
        for one in waits:
            one.wait_recv()

        @pl.when(chunk < y)
        def _():
            forward(chunk, False)

        return 0

    lax.fori_loop(5, 7, gather_end, 0)

    top = jnp.max(m_run[...], axis=0, keepdims=True)
    total = jnp.sum(l_run[...] * jnp.exp2(m_run[...] - top), axis=0, keepdims=True)
    lse[...] = jnp.broadcast_to(top + jnp.log2(total), lse.shape)
    lse_copy = copy(lse, lse_in, LSE, sibling)
    lse_copy.start()
    lse_copy.wait()
    high = jnp.maximum(lse[...], lse_in[...])
    low = jnp.minimum(lse[...], lse_in[...])
    lse[...] = high + jnp.log2(1.0 + jnp.exp2(low - high))

    def backward(chunk, diagonal):
        keys = kbuf[chunk].reshape(CHUNK, HEAD)
        vals = vbuf[chunk].reshape(CHUNK, HEAD)
        keys_t = keys.astype(F32).T.astype(BF16)
        for h in range(HEADS):
            cols = slice(h * ROWS, (h + 1) * ROWS)
            p = jnp.exp2(scores(keys, h, diagonal) - lse[0:1, cols])
            dp = dot(vals, do_t[:, cols])
            ds = (p * (dp - delta[0:1, cols]) * SCALE).astype(BF16)
            dv = dot(p.astype(BF16), dos[cols, :])
            dk = dot(ds, qs[cols, :])
            if h == 0:
                tmp_v[...] = dv
                tmp_k[...] = dk
            else:
                tmp_v[...] += dv
                tmp_k[...] += dk
            dq_t[:, cols] += dot(keys_t, ds)

    def sum_copies(t):
        target = dev(jnp.where(lax.rem(t, 2) == 0, at_y(1), at_y(-1)), z, core)
        return [
            copy(out.at[t], into.at[t], base + t, target)
            for out, into, base in ((out_v, in_v, SV), (out_k, in_k, SK))
        ]

    def reduce_step(t, _):
        s = t // 2
        chunk = jnp.where(lax.rem(t, 2) == 0, at_y(4 - s), at_y(s - 3))

        @pl.when(chunk < y)
        def _():
            backward(chunk, False)

        @pl.when(chunk > y)
        def _():
            tmp_v[...] = jnp.zeros(tmp_v.shape, F32)
            tmp_k[...] = jnp.zeros(tmp_k.shape, F32)

        @pl.when(t >= 2)
        def _():
            for one in sum_copies(t - 2):
                one.wait_recv()
            tmp_v[...] += in_v[t - 2].astype(F32)
            tmp_k[...] += in_k[t - 2].astype(F32)

        out_v[t] = tmp_v[...].astype(BF16)
        out_k[t] = tmp_k[...].astype(BF16)
        for one in sum_copies(t):
            one.start()
        return 0

    lax.fori_loop(0, 7, reduce_step, 0)
    backward(y, True)

    for h in range(HEADS):
        full = dq_t[:, h * ROWS : (h + 1) * ROWS].T.reshape(2, 128, HEAD)
        tmp_rows = pl.ds(h * ROWS, ROWS)
        p_rows = full.reshape(ROWS, HEAD)
        p_scr[pl.ds(0, ROWS), :] = p_rows
        dq_keep[h] = p_scr[pl.ds(pl.multiple_of(core * 128, 128), 128), :]
        dq_send[h] = p_scr[pl.ds(pl.multiple_of((1 - core) * 128, 128), 128), :]
    dq_copy = copy(dq_send, dq_in, DQ, sibling)
    dq_copy.start()

    for t in (5, 6):
        for one in sum_copies(t):
            one.wait_recv()
    tmp_v[...] += in_v[5].astype(F32) + in_v[6].astype(F32)
    tmp_k[...] += in_k[5].astype(F32) + in_k[6].astype(F32)

    zc = []
    for tmp, out, into, base in ((tmp_v, zout_v, zin_v, ZV), (tmp_k, zout_k, zin_k, ZK)):
        for i in range(1, Z):
            rows = pl.ds(pl.multiple_of(at_z(i) * 128, 128), 128)
            out[i - 1] = tmp[rows, :].astype(BF16)
            one = copy(out.at[i - 1], into.at[i - 1], base + i - 1, dev(y, at_z(i), core))
            one.start()
            zc.append(one)
    mine = pl.ds(pl.multiple_of(z * 128, 128), 128)
    for one in zc[:3]:
        one.wait_recv()
    value_grad = tmp_v[mine, :]
    for i in range(Z - 1):
        value_grad = value_grad + zin_v[i].astype(F32)
    value_low = value_grad.astype(BF16)
    dv_out[...] = value_low
    value_t = value_low.astype(F32).T.astype(BF16)

    def weight_step(i, _):
        for ref, half in ((w_keep, core), (w_send, 1 - core)):
            cols = pl.ds(pl.multiple_of(i * BLOCK_ROWS + half * 256, 256), 256)
            ref[i] = dot(value_t, x_ref[:, cols])
        return 0

    lax.fori_loop(0, Y, weight_step, 0)
    wc = copy(w_send, w_in, WC, sibling)
    wc.start()

    for one in zc[3:]:
        one.wait_recv()
    key_grad = tmp_k[mine, :]
    for i in range(Z - 1):
        key_grad = key_grad + zin_k[i].astype(F32)
    dk_out[...] = key_grad.astype(BF16)
    dq_copy.wait_recv()
    for h in range(HEADS):
        dq_out[:, h * HEAD : (h + 1) * HEAD] = (dq_keep[h] + dq_in[h]).astype(BF16)

    wc.wait_recv()
    wy = []
    for i in range(1, Y):
        target = at_y(i)
        wy_out[i - 1] = (w_keep[target] + w_in[target]).astype(BF16)
        one = copy(wy_out.at[i - 1], wy_in.at[i - 1], WY + i - 1, dev(target, z, core))
        one.start()
        wy.append(one)
    g = w_keep[y] + w_in[y]
    for i in range(1, Y):
        wy[i - 1].wait_recv()
        g = g + wy_in[i - 1].astype(F32)
    wz_out[...] = g.astype(BF16)
    wz = [copy(wz_out, wz_in.at[i - 1], WZ + i - 1, dev(y, at_z(i), core)) for i in range(1, Z)]
    for one in wz:
        one.start()
    for i in range(1, Z):
        wz[i - 1].wait_recv()
        g = g + wz_in[i - 1].astype(F32)
    g_out[...] = g
    gc = copy(g_out, g_in, GC, sibling)
    gc.start()
    gc.wait_recv()

    mine_g, other_g = g_out[...], g_in[...]
    gram = dot_high(mine_g, mine_g.T) + dot_high(other_g, other_g.T)
    eye = (
        lax.broadcasted_iota(jnp.int32, (HEAD, HEAD), 0) == lax.broadcasted_iota(jnp.int32, (HEAD, HEAD), 1)
    ).astype(F32)

    def all_sum(a):
        return jnp.sum(jnp.sum(a, axis=1, keepdims=True), axis=0, keepdims=True)

    squares = all_sum(gram * eye)
    gram_squares = all_sum(gram * gram)

    def inverse_root(size):
        shift = 0.1 * squares / size + 1e-06
        norm = jnp.sqrt(gram_squares + 2.0 * shift * squares + size * shift * shift)
        matrix = (gram + shift * eye) / norm
        root = None
        for iteration in range(NEWTON):
            factor = (5.0 * eye - matrix) * 0.25
            root = factor if root is None else dot_high(root, factor)
            if iteration < NEWTON - 1:
                square = dot_high(factor, factor)
                matrix = dot_high(dot_high(square, square), matrix)
        return root

    mixed = dot_high(inverse_root(BLOCK_ROWS), inverse_root(HEAD))
    first = pl.ds(pl.multiple_of(core * 256, 256), 256)
    second = pl.ds(pl.multiple_of((1 - core) * 256, 256), 256)
    p_mine = dot_high(mine_g.T, mixed)
    p_other = dot_high(other_g.T, mixed)
    p_scr[first, :] = p_mine
    p_scr[second, :] = p_other
    mean = (all_sum(p_mine * p_mine) + all_sum(p_other * p_other)) / (BLOCK_ROWS * HEAD)
    own = p_scr[pl.ds(pl.multiple_of((z * 2 + core) * 64, 64), 64), :]
    w_out[...] = (own / jnp.sqrt(mean + 1e-06)).astype(BF16)

    for one in kz + vz + sib + zc + wy + wz + [dq_copy, wc, gc]:
        one.wait_send()

    def finish(t, _):
        for one in ring_copies(t) + sum_copies(t):
            one.wait_send()
        return 0

    lax.fori_loop(0, 7, finish, 0)


def per_device(queries, keys, values, saved_out, grad_out, layer_in):
    vmem = pl.BlockSpec(memory_space=pltpu.VMEM)
    scratch = [
        pltpu.VMEM((Y, Z, 128, HEAD), BF16),
        pltpu.VMEM((Y, Z, 128, HEAD), BF16),
        pltpu.VMEM((ALL_ROWS, HEAD), BF16),
        pltpu.VMEM((ALL_ROWS, HEAD), BF16),
        pltpu.VMEM((ALL_ROWS, HEAD), BF16),
        pltpu.VMEM((HEAD, ALL_ROWS), BF16),
        pltpu.VMEM((HEAD, ALL_ROWS), BF16),
        pltpu.VMEM((8, ALL_ROWS), F32),
        pltpu.VMEM((8, ALL_ROWS), F32),
        pltpu.VMEM((8, ALL_ROWS), F32),
        pltpu.VMEM((8, ALL_ROWS), F32),
        pltpu.VMEM((8, ALL_ROWS), F32),
        pltpu.VMEM((HEAD, ALL_ROWS), F32),
        pltpu.VMEM((CHUNK, HEAD), F32),
        pltpu.VMEM((CHUNK, HEAD), F32),
        pltpu.VMEM((7, CHUNK, HEAD), BF16),
        pltpu.VMEM((7, CHUNK, HEAD), BF16),
        pltpu.VMEM((7, CHUNK, HEAD), BF16),
        pltpu.VMEM((7, CHUNK, HEAD), BF16),
        pltpu.VMEM((3, 128, HEAD), BF16),
        pltpu.VMEM((3, 128, HEAD), BF16),
        pltpu.VMEM((3, 128, HEAD), BF16),
        pltpu.VMEM((3, 128, HEAD), BF16),
        pltpu.VMEM((HEADS, 128, HEAD), F32),
        pltpu.VMEM((HEADS, 128, HEAD), F32),
        pltpu.VMEM((HEADS, 128, HEAD), F32),
        pltpu.VMEM((Y, HEAD, 256), F32),
        pltpu.VMEM((Y, HEAD, 256), F32),
        pltpu.VMEM((Y, HEAD, 256), F32),
        pltpu.VMEM((7, HEAD, 256), BF16),
        pltpu.VMEM((7, HEAD, 256), BF16),
        pltpu.VMEM((HEAD, 256), BF16),
        pltpu.VMEM((3, HEAD, 256), BF16),
        pltpu.VMEM((HEAD, 256), F32),
        pltpu.VMEM((HEAD, 256), F32),
        pltpu.VMEM((BLOCK_ROWS, HEAD), F32),
        pltpu.SemaphoreType.DMA((N_SEMS,)),
        pltpu.SemaphoreType.DMA((N_SEMS,)),
    ]
    shapes = (
        jax.ShapeDtypeStruct(queries.shape, BF16),
        jax.ShapeDtypeStruct(keys.shape, BF16),
        jax.ShapeDtypeStruct(values.shape, BF16),
        jax.ShapeDtypeStruct((64, HEAD), BF16),
    )
    return pl.pallas_call(
        kernel,
        out_shape=shapes,
        in_specs=[vmem] * 6,
        out_specs=(vmem,) * 4,
        scratch_shapes=scratch,
        compiler_params=pltpu.CompilerParams(
            collective_id=0, has_side_effects=True, vmem_limit_bytes=50 * 1024 * 1024
        ),
    )(queries, keys, values, saved_out, grad_out, layer_in)


def solution(mesh):
    placed = (P("ctx", "tp"),) * 5 + (P("ctx", None),)
    return jax.shard_map(
        per_device,
        mesh=mesh,
        in_specs=placed,
        out_specs=(P("ctx", "tp"),) * 4,
        check_vma=False,
    )
```

```python
import jax
import jax.numpy as jnp
from jax import lax
from jax.experimental import pallas as pl
from jax.experimental.pallas import tpu as pltpu
from jax.sharding import PartitionSpec as P

HEAD = 128
Y, Z = 8, 4
HEADS = 4
KEYS = 1024
NEWTON = 2
BLOCK_ROWS = 512
FILL = -1e30
SCALE = HEAD ** (-0.5)
SCALE2 = SCALE * 1.4426950408889634
HIGHEST = lax.Precision.HIGHEST
F32 = jnp.float32
BF16 = jnp.bfloat16
NT = (((1,), (1,)), ((), ()))

GROUPS = dict(
    KZ=3, VZ=3, KC=4, VC=4, RQ=7, RD=7, ST=7, XZ=3, DVC=1, ZV=3, VG=3, WC=1, WY=7, WZ=3, GC=1, RS=7, DKC=1, ZK=3
)
BASE, N_SEMS = {}, 0
for _name, _count in GROUPS.items():
    BASE[_name] = N_SEMS
    N_SEMS += _count


def dot(a, b, dims=(((1,), (0,)), ((), ())), precision=None):
    return lax.dot_general(a, b, dims, precision=precision, preferred_element_type=F32)


def dot_high(a, b, dims=(((1,), (0,)), ((), ()))):
    return dot(a, b, dims, precision=HIGHEST)


def kernel(
    q_ref, k_ref, v_ref, o_ref, do_ref, x_ref,
    dq_out, dk_out, dv_out, w_out,
    qs, dos, obuf, kl, vl, kt, xin, xs, xw, ptil,
    tops, stat, stat_in, factor, delta, dv_acc, dk_acc, tmp_q, out_q, in_q,
    dv_send, dv_in, dk_send, dk_in, zout_v, zin_v, zout_k, zin_k, vg,
    w_full, w_in, wk, wy_out, wy_in, gbuf, gbuf_in, gt, p_scr,
    send, recv, load,
):
    c = lax.axis_index("ctx")
    core = lax.rem(c, 2)
    z = lax.rem(c // 2, Z)
    y = c // (2 * Z)
    block = z * 2 + core

    def dev(yy, zz, cc):
        return {"ctx": (yy * Z + zz) * 2 + cc}

    sibling = dev(y, z, 1 - core)

    def at_y(step):
        return lax.rem(y + step + Y, Y)

    def at_z(step):
        return lax.rem(z + step, Z)

    def rows_of(number, size):
        return pl.ds(pl.multiple_of(number * size, size), size)

    sent = []

    def copy(src, dst, group, number, device):
        return pltpu.make_async_remote_copy(
            src_ref=src, dst_ref=dst, send_sem=send.at[BASE[group] + number], recv_sem=recv.at[BASE[group] + number],
            device_id=device, device_id_type=pl.DeviceIdType.MESH,
        )

    def start(copies):
        for one in copies:
            one.start()
            sent.append(one)
        return copies

    def wait_recv(copies):
        for one in copies:
            one.wait_recv()

    heads = [pl.ds(h * HEAD, HEAD) for h in range(HEADS)]
    pairs = [(k_ref, kl.at[rows_of(block, 128)])]
    pairs += [(q_ref.at[:, heads[h]], qs.at[y, h]) for h in range(HEADS)]
    pairs += [(do_ref.at[:, heads[h]], dos.at[y, h]) for h in range(HEADS)]
    pairs += [(v_ref, vl.at[rows_of(block, 128)])]
    pairs += [(o_ref.at[:, heads[h]], obuf.at[h]) for h in range(HEADS)]
    pairs += [(x_ref, xin)]
    loads = [pltpu.make_async_copy(src, dst, load.at[n]) for n, (src, dst) in enumerate(pairs)]
    for one in loads:
        one.start()

    barrier = pltpu.get_barrier_semaphore()
    partners = [dev(at_y(i), z, core) for i in range(1, Y)]
    partners += [dev(y, at_z(i), core) for i in range(1, Z)] + [sibling]
    for partner in partners:
        pl.semaphore_signal(barrier, inc=1, device_id=partner, device_id_type=pl.DeviceIdType.MESH)
    for one in loads[:5]:
        one.wait()
    pl.semaphore_wait(barrier, len(partners))

    def ring_target(t):
        return dev(jnp.where(lax.rem(t, 2) == 0, at_y(1), at_y(-1)), z, core)

    def ring_copy(buf, group, t):
        chunk = jnp.where(lax.rem(t, 2) == 0, at_y(-(t // 2)), at_y(t // 2))
        return copy(buf.at[chunk], buf.at[chunk], group, t, ring_target(t))

    def ring_arrival(t):
        return jnp.where(lax.rem(t, 2) == 0, at_y(-1 - t // 2), at_y(1 + t // 2))

    def ring_wait(buf, group, t):
        chunk = ring_arrival(t)
        copy(buf.at[chunk], buf.at[chunk], group, t, sibling).wait_recv()

    def block_copies(buf, group):
        mine = buf.at[rows_of(block, 128)]
        return [copy(mine, mine, group, i - 1, dev(y, at_z(i), core)) for i in range(1, Z)]

    def core_copy(buf, group, i):
        rows = rows_of(at_z(i) * 2 + core, 128)
        return copy(buf.at[rows], buf.at[rows], group, i, sibling)

    def arrived_block(buf, group, i):
        rows = rows_of(at_z(Z - i) * 2 + core, 128)
        copy(buf.at[rows], buf.at[rows], group, i - 1, sibling).wait_recv()

    def core_wait(buf, group, i):
        rows = rows_of(at_z(i) * 2 + 1 - core, 128)
        copy(buf.at[rows], buf.at[rows], group, i, sibling).wait_recv()

    start(block_copies(kl, "KZ"))
    for t in range(2):
        ring_copy(qs, "RQ", t).start()
    start([core_copy(kl, "KC", 0)])
    for one in loads[5:]:
        one.wait()
    start(block_copies(vl, "VZ"))
    start([core_copy(vl, "VC", 0)])

    stat[...] = jnp.full(stat.shape, FILL, F32)
    tops[...] = jnp.full(tops.shape, FILL, F32)
    dv_acc[...] = jnp.zeros(dv_acc.shape, F32)
    dk_acc[...] = jnp.zeros(dk_acc.shape, F32)
    for h in range(HEADS):
        product = dos[y, h].astype(F32) * obuf[h].astype(F32)
        stat[8:9, h * HEAD : (h + 1) * HEAD] = jnp.sum(product.T, axis=0, keepdims=True)

    def arrange(i, _):
        for zz in range(Z):
            xs[zz, :, rows_of(i, 128)] = xin[:, rows_of(i * Z + zz, 128)]
        return 0

    lax.fori_loop(0, Y, arrange, 0)

    for i in range(1, Z):
        arrived_block(kl, "KZ", i)
        start([core_copy(kl, "KC", Z - i)])
    for i in range(Z):
        core_wait(kl, "KC", i)

    def row_of(ref, chunk, cols):
        number = lax.broadcasted_iota(jnp.int32, (Y, 256), 0)
        return jnp.sum(jnp.where(number == chunk, ref[0:Y, cols], 0.0), axis=0, keepdims=True)

    def put_row(ref, chunk, cols, row):
        number = lax.broadcasted_iota(jnp.int32, (Y, 256), 0)
        ref[0:Y, cols] = jnp.where(number == chunk, row, ref[0:Y, cols])

    halves = [slice(0, 256), slice(256, 512)]

    def forward(chunk, diagonal):
        for n, cols in enumerate(halves):
            q2 = qs[chunk, 2 * n : 2 * n + 2].reshape(256, HEAD)
            s = dot(kl[...], q2, NT) * SCALE2
            if diagonal:
                key = lax.broadcasted_iota(jnp.int32, (KEYS, 256), 0)
                row = (lax.broadcasted_iota(jnp.int32, (KEYS, 256), 1) & 127) + block * 128
                s = jnp.where(key <= row, s, FILL)
            top = jnp.max(s, axis=0, keepdims=True)
            e = jnp.exp2(s - top)
            ptil[chunk, n] = e
            put_row(tops, chunk, cols, top)
            put_row(stat, chunk, cols, top + jnp.log2(jnp.sum(e, axis=0, keepdims=True)))

    def gather_step(t, _):
        @pl.when(t >= 2)
        def _():
            ring_wait(qs, "RQ", t - 2)
            ring_copy(qs, "RQ", t).start()

        @pl.when(t == 1)
        def _():
            forward(y, True)

        @pl.when(t >= 2)
        def _():
            chunk = ring_arrival(t - 2)

            @pl.when(chunk > y)
            def _():
                forward(chunk, False)

        return 0

    lax.fori_loop(1, 7, gather_step, 0)
    for t in range(2):
        ring_copy(dos, "RD", t).start()
    xz = start([copy(xs.at[at_z(i)], xw.at[z], "XZ", i - 1, dev(y, at_z(i), core)) for i in range(1, Z)])
    xw[z] = xs[z]
    for i in range(1, Z):
        arrived_block(vl, "VZ", i)
        start([core_copy(vl, "VC", Z - i)])

    def gather_end(t, _):
        ring_wait(qs, "RQ", t)
        chunk = ring_arrival(t)

        @pl.when(chunk > y)
        def _():
            forward(chunk, False)

        return 0

    lax.fori_loop(5, 7, gather_end, 0)

    st = start([copy(stat, stat_in.at[i - 1], "ST", i - 1, dev(at_y(i), z, core)) for i in range(1, Y)])
    for t in range(2):
        ring_wait(dos, "RD", t)
        ring_copy(dos, "RD", t + 2).start()
    kt[...] = kl[...].astype(F32).T.astype(BF16)
    wait_recv(st)
    parts = [stat[0:8, :]] + [stat_in[i, 0:8, :] for i in range(Y - 1)]
    high = parts[0]
    for part in parts[1:]:
        high = jnp.maximum(high, part)
    total = sum(jnp.exp2(part - high) for part in parts)
    factor[...] = jnp.exp2(tops[...] - (high + jnp.log2(total)))
    number = lax.broadcasted_iota(jnp.int32, (Y, 512), 0)
    all_delta = jnp.where(number == y, stat[8:9, :], 0.0)
    for i in range(1, Y):
        all_delta = jnp.where(number == at_y(Y - i), stat_in[i - 1, 8:9, :], all_delta)
    delta[...] = all_delta

    def value_tile(chunk):
        for n, cols in enumerate(halves):
            p = (ptil[chunk, n] * row_of(factor, chunk, cols)).astype(BF16)
            dv_acc[...] += dot(p, dos[chunk, 2 * n : 2 * n + 2].reshape(256, HEAD))

    def value_step(n, _):
        t = jnp.maximum(n - 1, 0)

        @pl.when(n >= 3)
        def _():
            ring_wait(dos, "RD", t)

        @pl.when(jnp.logical_and(n >= 3, n < 6))
        def _():
            ring_copy(dos, "RD", t + 2).start()

        chunk = jnp.where(n == 0, y, ring_arrival(t))

        @pl.when(chunk >= y)
        def _():
            value_tile(chunk)

        return 0

    lax.fori_loop(0, 8, value_step, 0)

    def split_cores(acc, out):
        for zz in range(Z):
            out[zz] = acc[rows_of(zz * 2 + 1 - core, 128), :]

    def z_sums(acc, got, out, into, group):
        copies = []
        for i in range(1, Z):
            zz = at_z(i)
            out[i - 1] = (acc[rows_of(zz * 2 + core, 128), :] + got[zz]).astype(BF16)
            copies.append(copy(out.at[i - 1], into.at[i - 1], group, i - 1, dev(y, zz, core)))
        return copies

    def z_total(acc, got, into):
        total = acc[rows_of(block, 128), :] + got[z]
        for i in range(Z - 1):
            total = total + into[i].astype(F32)
        return total.astype(BF16)

    split_cores(dv_acc, dv_send)
    dvc = start([copy(dv_send, dv_in, "DVC", 0, sibling)])

    zv = [copy(zout_v.at[i - 1], zin_v.at[i - 1], "ZV", i - 1, dev(y, at_z(i), core)) for i in range(1, Z)]
    vgc = [copy(vg.at[z], vg.at[z], "VG", i - 1, dev(y, at_z(i), core)) for i in range(1, Z)]
    wc = [copy(w_full.at[rows_of(1 - core, 64)], w_in, "WC", 0, sibling)]
    wy = [copy(wy_out.at[i - 1], wy_in.at[i - 1], "WY", i - 1, dev(at_y(i), z, core)) for i in range(1, Y)]

    def chain_1():
        wait_recv(dvc)
        z_sums(dv_acc, dv_in, zout_v, zin_v, "ZV")
        start(zv)

    def chain_2():
        wait_recv(zv)
        vg[z] = z_total(dv_acc, dv_in, zin_v)
        start(vgc)
        dv_out[...] = vg[z]

    def chain_3():
        wait_recv(vgc)
        wait_recv(xz)
        value_t = vg[...].reshape(512, HEAD).astype(F32).T.astype(BF16)
        for n in range(4):
            cols = slice(n * 256, (n + 1) * 256)
            w_full[:, cols] = dot(value_t, xw[:, :, cols].reshape(512, 256))
        start(wc)

    def chain_4():
        wait_recv(wc)
        kept = w_full[rows_of(core, 64), :] + w_in[...]
        for i in range(Y):
            wk[i] = kept[:, i * 128 : (i + 1) * 128]
        for i in range(1, Y):
            wy_out[i - 1] = wk[at_y(i)].astype(BF16)
        start(wy)

    def tile(chunk):
        for n, cols in enumerate(halves):
            q2 = qs[chunk, 2 * n : 2 * n + 2].reshape(256, HEAD)
            do2 = dos[chunk, 2 * n : 2 * n + 2].reshape(256, HEAD)
            p = ptil[chunk, n] * row_of(factor, chunk, cols)
            dp = dot(vl[...], do2, NT)
            ds = (p * (dp - row_of(delta, chunk, cols)) * SCALE).astype(BF16)
            dk_acc[...] += dot(ds, q2)
            tmp_q[:, cols] = dot(kt[...], ds)

    def sum_copy(t):
        return copy(out_q.at[t], in_q.at[t], "RS", t, ring_target(t))

    for i in range(Z):
        core_wait(vl, "VC", i)

    def tile_step(t, _):
        s = t // 2
        chunk = jnp.where(t == 7, y, jnp.where(lax.rem(t, 2) == 0, at_y(4 - s), at_y(s - 3)))

        @pl.when(chunk >= y)
        def _():
            tile(chunk)

        @pl.when(chunk < y)
        def _():
            tmp_q[...] = jnp.zeros(tmp_q.shape, F32)

        @pl.when(jnp.logical_and(t >= 2, t < 7))
        def _():
            sum_copy(t - 2).wait_recv()
            tmp_q[...] += in_q[t - 2].astype(F32)

        @pl.when(t < 7)
        def _():
            out_q[t] = tmp_q[...].astype(BF16)
            sum_copy(t).start()

        for when, chain in ((0, chain_1), (2, chain_2), (4, chain_3), (5, chain_4)):
            pl.when(t == when)(chain)
        return 0

    lax.fori_loop(0, 8, tile_step, 0)

    split_cores(dk_acc, dk_send)
    dkc = start([copy(dk_send, dk_in, "DKC", 0, sibling)])

    wait_recv(wy)
    g = wk[y]
    for i in range(Y - 1):
        g = g + wy_in[i].astype(F32)
    gbuf[z] = g
    wz = start([copy(gbuf.at[z], gbuf.at[z], "WZ", i - 1, dev(y, at_z(i), core)) for i in range(1, Z)])

    wait_recv(dkc)
    zk = start(z_sums(dk_acc, dk_in, zout_k, zin_k, "ZK"))

    wait_recv(wz)
    gc = start([copy(gbuf, gbuf_in, "GC", 0, sibling)])

    for t in (5, 6):
        sum_copy(t).wait_recv()
    tmp_q[...] += in_q[5].astype(F32) + in_q[6].astype(F32)
    for h in range(HEADS):
        dq_out[:, h * HEAD : (h + 1) * HEAD] = tmp_q[:, h * HEAD : (h + 1) * HEAD].T.astype(BF16)

    wait_recv(gc)
    for zz in range(Z):
        gt[rows_of(core, 64), zz * 128 : (zz + 1) * 128] = gbuf[zz]
        gt[rows_of(1 - core, 64), zz * 128 : (zz + 1) * 128] = gbuf_in[zz]

    grad_t = gt[...]
    gram = dot_high(grad_t, grad_t, NT)
    eye = (
        lax.broadcasted_iota(jnp.int32, (HEAD, HEAD), 0) == lax.broadcasted_iota(jnp.int32, (HEAD, HEAD), 1)
    ).astype(F32)

    def all_sum(a):
        return jnp.sum(jnp.sum(a, axis=0, keepdims=True), axis=1, keepdims=True)

    squares = all_sum(gram * eye)
    gram_squares = all_sum(gram * gram)

    def inverse_root(size):
        shift = 0.1 * squares / size + 1e-06
        norm = jnp.sqrt(gram_squares + 2.0 * shift * squares + size * shift * shift)
        matrix = (gram + shift * eye) / norm
        root = None
        for iteration in range(NEWTON):
            part = (5.0 * eye - matrix) * 0.25
            root = part if root is None else dot_high(root, part)
            if iteration < NEWTON - 1:
                square = dot_high(part, part)
                matrix = dot_high(dot_high(square, square), matrix)
        return root

    mixed = dot_high(inverse_root(BLOCK_ROWS), inverse_root(HEAD))
    precond_t = dot_high(mixed, grad_t)
    mean = all_sum(precond_t * precond_t) / (BLOCK_ROWS * HEAD)
    p_scr[...] = (precond_t / jnp.sqrt(mean + 1e-06)).T
    w_out[...] = p_scr[rows_of(block, 64), :].astype(BF16)

    wait_recv(zk)
    dk_out[...] = z_total(dk_acc, dk_in, zin_k)

    for one in sent:
        one.wait_send()

    def finish(t, _):
        for one in (ring_copy(qs, "RQ", t), ring_copy(dos, "RD", t), sum_copy(t)):
            one.wait_send()
        return 0

    lax.fori_loop(0, 7, finish, 0)


def per_device(queries, keys, values, saved_out, grad_out, layer_in):
    vmem = pl.BlockSpec(memory_space=pltpu.VMEM)
    hbm = pl.BlockSpec(memory_space=pl.ANY)
    row_chunk = (HEADS, 128, HEAD)
    scratch = [
        pltpu.VMEM((Y,) + row_chunk, BF16),
        pltpu.VMEM((Y,) + row_chunk, BF16),
        pltpu.VMEM(row_chunk, BF16),
        pltpu.VMEM((KEYS, HEAD), BF16),
        pltpu.VMEM((KEYS, HEAD), BF16),
        pltpu.VMEM((HEAD, KEYS), BF16),
        pltpu.VMEM((128, 4096), BF16),
        pltpu.VMEM((Z, 128, 1024), BF16),
        pltpu.VMEM((Z, 128, 1024), BF16),
        pltpu.VMEM((Y, 2, KEYS, 256), F32),
        pltpu.VMEM((Y, 512), F32),
        pltpu.VMEM((16, 512), F32),
        pltpu.VMEM((Y - 1, 16, 512), F32),
        pltpu.VMEM((Y, 512), F32),
        pltpu.VMEM((Y, 512), F32),
        pltpu.VMEM((KEYS, HEAD), F32),
        pltpu.VMEM((KEYS, HEAD), F32),
        pltpu.VMEM((HEAD, 512), F32),
        pltpu.VMEM((7, HEAD, 512), BF16),
        pltpu.VMEM((7, HEAD, 512), BF16),
        pltpu.VMEM((Z, 128, HEAD), F32),
        pltpu.VMEM((Z, 128, HEAD), F32),
        pltpu.VMEM((Z, 128, HEAD), F32),
        pltpu.VMEM((Z, 128, HEAD), F32),
        pltpu.VMEM((3, 128, HEAD), BF16),
        pltpu.VMEM((3, 128, HEAD), BF16),
        pltpu.VMEM((3, 128, HEAD), BF16),
        pltpu.VMEM((3, 128, HEAD), BF16),
        pltpu.VMEM((Z, 128, HEAD), BF16),
        pltpu.VMEM((HEAD, 1024), F32),
        pltpu.VMEM((64, 1024), F32),
        pltpu.VMEM((Y, 64, 128), F32),
        pltpu.VMEM((7, 64, 128), BF16),
        pltpu.VMEM((7, 64, 128), BF16),
        pltpu.VMEM((Z, 64, 128), F32),
        pltpu.VMEM((Z, 64, 128), F32),
        pltpu.VMEM((HEAD, BLOCK_ROWS), F32),
        pltpu.VMEM((BLOCK_ROWS, HEAD), F32),
        pltpu.SemaphoreType.DMA((N_SEMS,)),
        pltpu.SemaphoreType.DMA((N_SEMS,)),
        pltpu.SemaphoreType.DMA((15,)),
    ]
    shapes = (
        jax.ShapeDtypeStruct(queries.shape, BF16),
        jax.ShapeDtypeStruct(keys.shape, BF16),
        jax.ShapeDtypeStruct(values.shape, BF16),
        jax.ShapeDtypeStruct((64, HEAD), BF16),
    )
    return pl.pallas_call(
        kernel,
        out_shape=shapes,
        in_specs=[hbm] * 6,
        out_specs=(vmem,) * 4,
        scratch_shapes=scratch,
        compiler_params=pltpu.CompilerParams(
            collective_id=0, has_side_effects=True, vmem_limit_bytes=60 * 1024 * 1024
        ),
    )(queries, keys, values, saved_out, grad_out, layer_in)


def solution(mesh):
    placed = (P("ctx", "tp"),) * 5 + (P("ctx", None),)
    return jax.shard_map(
        per_device,
        mesh=mesh,
        in_specs=placed,
        out_specs=(P("ctx", "tp"),) * 4,
        check_vma=False,
    )
```

```python
import jax
import jax.numpy as jnp
from jax import lax
from jax.experimental import pallas as pl
from jax.experimental.pallas import tpu as pltpu
from jax.sharding import PartitionSpec as P

HEAD = 128
Y, Z = 8, 4
HEADS = 4
KEYS = 1024
NEWTON = 2
BLOCK_ROWS = 512
FILL = -1e30
SCALE = HEAD ** (-0.5)
SCALE2 = SCALE * 1.4426950408889634
HIGHEST = lax.Precision.HIGHEST
F32 = jnp.float32
BF16 = jnp.bfloat16
NT = (((1,), (1,)), ((), ()))

GROUPS = dict(
    KZ=3, VZ=3, KC=4, VC=4, RQ=7, RD=7, ST=7, XZ=3, DVC=1, ZV=3, VG=3, WC=1, WY=7, WZ=3, GC=1, RS=7, DKC=1, ZK=3
)
BASE, N_SEMS = {}, 0
for _name, _count in GROUPS.items():
    BASE[_name] = N_SEMS
    N_SEMS += _count


def dot(a, b, dims=(((1,), (0,)), ((), ())), precision=None):
    return lax.dot_general(a, b, dims, precision=precision, preferred_element_type=F32)


def dot_high(a, b, dims=(((1,), (0,)), ((), ()))):
    return dot(a, b, dims, precision=HIGHEST)


def kernel(
    q_ref, k_ref, v_ref, o_ref, do_ref, x_ref,
    dq_out, dk_out, dv_out, w_out,
    qs, dos, obuf, kl, vl, kt, xin, xs, xw, ptil,
    tops, stat, stat_in, factor, delta, dv_acc, dk_acc, tmp_q, out_q, in_q,
    dv_send, dv_in, dk_send, dk_in, zout_v, zin_v, zout_k, zin_k, vg,
    w_full, w_in, wk, wy_out, wy_in, gbuf, gbuf_in, gt, p_scr,
    send, recv, load,
):
    c = lax.axis_index("ctx")
    core = lax.rem(c, 2)
    z = lax.rem(c // 2, Z)
    y = c // (2 * Z)
    block = z * 2 + core

    def dev(yy, zz, cc):
        return {"ctx": (yy * Z + zz) * 2 + cc}

    sibling = dev(y, z, 1 - core)

    def at_y(step):
        return lax.rem(y + step + Y, Y)

    def at_z(step):
        return lax.rem(z + step, Z)

    def rows_of(number, size):
        return pl.ds(pl.multiple_of(number * size, size), size)

    sent = []

    def copy(src, dst, group, number, device):
        return pltpu.make_async_remote_copy(
            src_ref=src, dst_ref=dst, send_sem=send.at[BASE[group] + number], recv_sem=recv.at[BASE[group] + number],
            device_id=device, device_id_type=pl.DeviceIdType.MESH,
        )

    def start(copies):
        for one in copies:
            one.start()
            sent.append(one)
        return copies

    def wait_recv(copies):
        for one in copies:
            one.wait_recv()

    heads = [pl.ds(h * HEAD, HEAD) for h in range(HEADS)]
    pairs = [(k_ref, kl.at[rows_of(block, 128)])]
    pairs += [(q_ref.at[:, heads[h]], qs.at[y, h]) for h in range(HEADS)]
    pairs += [(do_ref.at[:, heads[h]], dos.at[y, h]) for h in range(HEADS)]
    pairs += [(v_ref, vl.at[rows_of(block, 128)])]
    pairs += [(o_ref.at[:, heads[h]], obuf.at[h]) for h in range(HEADS)]
    pairs += [(x_ref, xin)]
    loads = [pltpu.make_async_copy(src, dst, load.at[n]) for n, (src, dst) in enumerate(pairs)]
    for one in loads:
        one.start()

    barrier = pltpu.get_barrier_semaphore()
    partners = [dev(at_y(i), z, core) for i in range(1, Y)]
    partners += [dev(y, at_z(i), core) for i in range(1, Z)] + [sibling]
    for partner in partners:
        pl.semaphore_signal(barrier, inc=1, device_id=partner, device_id_type=pl.DeviceIdType.MESH)
    for one in loads[:5]:
        one.wait()
    pl.semaphore_wait(barrier, len(partners))

    def ring_target(t):
        return dev(jnp.where(lax.rem(t, 2) == 0, at_y(1), at_y(-1)), z, core)

    def ring_copy(buf, group, t):
        chunk = jnp.where(lax.rem(t, 2) == 0, at_y(-(t // 2)), at_y(t // 2))
        return copy(buf.at[chunk], buf.at[chunk], group, t, ring_target(t))

    def ring_arrival(t):
        return jnp.where(lax.rem(t, 2) == 0, at_y(-1 - t // 2), at_y(1 + t // 2))

    def ring_wait(buf, group, t):
        chunk = ring_arrival(t)
        copy(buf.at[chunk], buf.at[chunk], group, t, sibling).wait_recv()

    def block_copies(buf, group):
        mine = buf.at[rows_of(block, 128)]
        return [copy(mine, mine, group, i - 1, dev(y, at_z(i), core)) for i in range(1, Z)]

    def core_copy(buf, group, i):
        rows = rows_of(at_z(i) * 2 + core, 128)
        return copy(buf.at[rows], buf.at[rows], group, i, sibling)

    def arrived_block(buf, group, i):
        rows = rows_of(at_z(Z - i) * 2 + core, 128)
        copy(buf.at[rows], buf.at[rows], group, i - 1, sibling).wait_recv()

    def core_wait(buf, group, i):
        rows = rows_of(at_z(i) * 2 + 1 - core, 128)
        copy(buf.at[rows], buf.at[rows], group, i, sibling).wait_recv()

    start(block_copies(kl, "KZ"))
    for t in range(2):
        ring_copy(qs, "RQ", t).start()
    start([core_copy(kl, "KC", 0)])
    for one in loads[5:9]:
        one.wait()
    for t in range(2):
        ring_copy(dos, "RD", t).start()
    for one in loads[9:]:
        one.wait()
    start(block_copies(vl, "VZ"))
    start([core_copy(vl, "VC", 0)])

    stat[...] = jnp.full(stat.shape, FILL, F32)
    tops[...] = jnp.full(tops.shape, FILL, F32)
    dv_acc[...] = jnp.zeros(dv_acc.shape, F32)
    dk_acc[...] = jnp.zeros(dk_acc.shape, F32)
    for h in range(HEADS):
        product = dos[y, h].astype(F32) * obuf[h].astype(F32)
        stat[8:9, h * HEAD : (h + 1) * HEAD] = jnp.sum(product.T, axis=0, keepdims=True)

    def arrange(i, _):
        for zz in range(Z):
            xs[zz, :, rows_of(i, 128)] = xin[:, rows_of(i * Z + zz, 128)]
        return 0

    lax.fori_loop(0, Y, arrange, 0)

    for i in range(1, Z):
        arrived_block(kl, "KZ", i)
        start([core_copy(kl, "KC", Z - i)])

    def row_of(ref, chunk, cols):
        number = lax.broadcasted_iota(jnp.int32, (Y, 256), 0)
        return jnp.sum(jnp.where(number == chunk, ref[0:Y, cols], 0.0), axis=0, keepdims=True)

    def put_row(ref, chunk, cols, row):
        number = lax.broadcasted_iota(jnp.int32, (Y, 256), 0)
        ref[0:Y, cols] = jnp.where(number == chunk, row, ref[0:Y, cols])

    halves = [slice(0, 256), slice(256, 512)]

    def forward(chunk, diagonal):
        for n, cols in enumerate(halves):
            q2 = qs[chunk, 2 * n : 2 * n + 2].reshape(256, HEAD)
            s = dot(kl[...], q2, NT) * SCALE2
            if diagonal:
                key = lax.broadcasted_iota(jnp.int32, (KEYS, 256), 0)
                row = (lax.broadcasted_iota(jnp.int32, (KEYS, 256), 1) & 127) + block * 128
                s = jnp.where(key <= row, s, FILL)
            top = jnp.max(s, axis=0, keepdims=True)
            e = jnp.exp2(s - top)
            ptil[chunk, n] = e
            put_row(tops, chunk, cols, top)
            put_row(stat, chunk, cols, top + jnp.log2(jnp.sum(e, axis=0, keepdims=True)))

    def pass_on(buf, group, t):
        ring_wait(buf, group, t)

        @pl.when(t + 1 < 7)
        def _():
            ring_wait(buf, group, t + 1)

        @pl.when(t + 2 < 7)
        def _():
            ring_copy(buf, group, t + 2).start()

        @pl.when(t + 3 < 7)
        def _():
            ring_copy(buf, group, t + 3).start()

    def gather_step(n, _):
        t = jnp.maximum(n - 1, 0)

        @pl.when(jnp.logical_or(n == 0, jnp.logical_and(n > 1, lax.rem(t, 2) == 0)))
        def _():
            pass_on(qs, "RQ", t)

        @pl.when(n == 0)
        def _():
            for i in range(Z):
                core_wait(kl, "KC", i)
            forward(y, True)

        @pl.when(jnp.logical_or(n == 0, jnp.logical_and(n > 2, lax.rem(n, 2) == 0)))
        def _():
            pass_on(dos, "RD", jnp.maximum(n - 2, 0))

        @pl.when(n == 2)
        def _():
            for i in range(1, Z):
                arrived_block(vl, "VZ", i)
                start([vc[Z - i]])
            start(xz)

        chunk = ring_arrival(t)

        @pl.when(jnp.logical_and(n > 0, chunk > y))
        def _():
            forward(chunk, False)

        return 0

    xz = [copy(xs.at[at_z(i)], xw.at[z], "XZ", i - 1, dev(y, at_z(i), core)) for i in range(1, Z)]
    xw[z] = xs[z]
    vc = [core_copy(vl, "VC", i) for i in range(Z)]
    lax.fori_loop(0, 8, gather_step, 0)

    st = start([copy(stat, stat_in.at[i - 1], "ST", i - 1, dev(at_y(i), z, core)) for i in range(1, Y)])
    ring_wait(dos, "RD", 6)
    kt[...] = kl[...].astype(F32).T.astype(BF16)
    wait_recv(st)
    parts = [stat[0:8, :]] + [stat_in[i, 0:8, :] for i in range(Y - 1)]
    high = parts[0]
    for part in parts[1:]:
        high = jnp.maximum(high, part)
    total = sum(jnp.exp2(part - high) for part in parts)
    factor[...] = jnp.exp2(tops[...] - (high + jnp.log2(total)))
    number = lax.broadcasted_iota(jnp.int32, (Y, 512), 0)
    all_delta = jnp.where(number == y, stat[8:9, :], 0.0)
    for i in range(1, Y):
        all_delta = jnp.where(number == at_y(Y - i), stat_in[i - 1, 8:9, :], all_delta)
    delta[...] = all_delta

    def value_tile(chunk):
        for n, cols in enumerate(halves):
            p = (ptil[chunk, n] * row_of(factor, chunk, cols)).astype(BF16)
            dv_acc[...] += dot(p, dos[chunk, 2 * n : 2 * n + 2].reshape(256, HEAD))

    def value_step(n, _):
        chunk = jnp.where(n == 0, y, ring_arrival(jnp.maximum(n - 1, 0)))

        @pl.when(chunk >= y)
        def _():
            value_tile(chunk)

        return 0

    lax.fori_loop(0, 8, value_step, 0)

    def split_cores(acc, out):
        for zz in range(Z):
            out[zz] = acc[rows_of(zz * 2 + 1 - core, 128), :]

    def z_sums(acc, got, out, into, group):
        copies = []
        for i in range(1, Z):
            zz = at_z(i)
            out[i - 1] = (acc[rows_of(zz * 2 + core, 128), :] + got[zz]).astype(BF16)
            copies.append(copy(out.at[i - 1], into.at[i - 1], group, i - 1, dev(y, zz, core)))
        return copies

    def z_total(acc, got, into):
        total = acc[rows_of(block, 128), :] + got[z]
        for i in range(Z - 1):
            total = total + into[i].astype(F32)
        return total.astype(BF16)

    split_cores(dv_acc, dv_send)
    dvc = start([copy(dv_send, dv_in, "DVC", 0, sibling)])

    zv = [copy(zout_v.at[i - 1], zin_v.at[i - 1], "ZV", i - 1, dev(y, at_z(i), core)) for i in range(1, Z)]
    vgc = [copy(vg.at[z], vg.at[z], "VG", i - 1, dev(y, at_z(i), core)) for i in range(1, Z)]
    wc = [copy(w_full.at[rows_of(1 - core, 64)], w_in, "WC", 0, sibling)]
    wy = [copy(wy_out.at[i - 1], wy_in.at[i - 1], "WY", i - 1, dev(at_y(i), z, core)) for i in range(1, Y)]

    wz = [copy(gbuf.at[z], gbuf.at[z], "WZ", i - 1, dev(y, at_z(i), core)) for i in range(1, Z)]
    gc = [copy(gbuf, gbuf_in, "GC", 0, sibling)]

    def chain_1():
        wait_recv(dvc)
        z_sums(dv_acc, dv_in, zout_v, zin_v, "ZV")
        start(zv)

    def chain_2():
        wait_recv(zv)
        vg[z] = z_total(dv_acc, dv_in, zin_v)
        start(vgc)
        dv_out[...] = vg[z]

    def chain_3():
        wait_recv(vgc)
        wait_recv(xz)
        value_t = vg[...].reshape(512, HEAD).astype(F32).T.astype(BF16)
        for n in range(4):
            cols = slice(n * 256, (n + 1) * 256)
            w_full[:, cols] = dot(value_t, xw[:, :, cols].reshape(512, 256))
        start(wc)

    def chain_4():
        wait_recv(wc)
        kept = w_full[rows_of(core, 64), :] + w_in[...]
        for i in range(Y):
            wk[i] = kept[:, i * 128 : (i + 1) * 128]
        for i in range(1, Y):
            wy_out[i - 1] = wk[at_y(i)].astype(BF16)
        start(wy)

    def chain_5():
        wait_recv(wy)
        g = wk[y]
        for i in range(Y - 1):
            g = g + wy_in[i].astype(F32)
        gbuf[z] = g
        start(wz)

    def chain_6():
        wait_recv(wz)
        start(gc)

    def tile(chunk):
        for n, cols in enumerate(halves):
            q2 = qs[chunk, 2 * n : 2 * n + 2].reshape(256, HEAD)
            do2 = dos[chunk, 2 * n : 2 * n + 2].reshape(256, HEAD)
            p = ptil[chunk, n] * row_of(factor, chunk, cols)
            dp = dot(vl[...], do2, NT)
            ds = (p * (dp - row_of(delta, chunk, cols)) * SCALE).astype(BF16)
            dk_acc[...] += dot(ds, q2)
            tmp_q[:, cols] = dot(kt[...], ds)

    def sum_copy(t):
        return copy(out_q.at[t], in_q.at[t], "RS", t, ring_target(t))

    for i in range(Z):
        core_wait(vl, "VC", i)

    def tile_step(t, _):
        s = t // 2
        chunk = jnp.where(t == 7, y, jnp.where(lax.rem(t, 2) == 0, at_y(4 - s), at_y(s - 3)))

        @pl.when(chunk >= y)
        def _():
            tile(chunk)

        @pl.when(chunk < y)
        def _():
            tmp_q[...] = jnp.zeros(tmp_q.shape, F32)

        for when, chain in ((2, chain_2), (4, chain_4), (6, chain_5)):
            pl.when(t == when)(chain)

        @pl.when(jnp.logical_and(t >= 2, t < 7))
        def _():
            sum_copy(t - 2).wait_recv()
            tmp_q[...] += in_q[t - 2].astype(F32)

        @pl.when(t < 7)
        def _():
            out_q[t] = tmp_q[...].astype(BF16)
            sum_copy(t).start()

        for when, chain in ((0, chain_1), (3, chain_3), (7, chain_6)):
            pl.when(t == when)(chain)
        return 0

    lax.fori_loop(0, 8, tile_step, 0)

    split_cores(dk_acc, dk_send)
    dkc = start([copy(dk_send, dk_in, "DKC", 0, sibling)])
    wait_recv(dkc)
    zk = start(z_sums(dk_acc, dk_in, zout_k, zin_k, "ZK"))

    wait_recv(gc)
    for zz in range(Z):
        gt[rows_of(core, 64), zz * 128 : (zz + 1) * 128] = gbuf[zz]
        gt[rows_of(1 - core, 64), zz * 128 : (zz + 1) * 128] = gbuf_in[zz]

    grad_t = gt[...]
    gram = dot_high(grad_t, grad_t, NT)
    eye = (
        lax.broadcasted_iota(jnp.int32, (HEAD, HEAD), 0) == lax.broadcasted_iota(jnp.int32, (HEAD, HEAD), 1)
    ).astype(F32)

    def all_sum(a):
        return jnp.sum(jnp.sum(a, axis=0, keepdims=True), axis=1, keepdims=True)

    squares = all_sum(gram * eye)
    gram_squares = all_sum(gram * gram)

    def inverse_root(size):
        shift = 0.1 * squares / size + 1e-06
        norm = jnp.sqrt(gram_squares + 2.0 * shift * squares + size * shift * shift)
        matrix = (gram + shift * eye) / norm
        root = None
        for iteration in range(NEWTON):
            part = (5.0 * eye - matrix) * 0.25
            root = part if root is None else dot_high(root, part)
            if iteration < NEWTON - 1:
                square = dot_high(part, part)
                matrix = dot_high(dot_high(square, square), matrix)
        return root

    mixed = dot_high(inverse_root(BLOCK_ROWS), inverse_root(HEAD))
    precond_t = dot_high(mixed, grad_t)
    mean = all_sum(precond_t * precond_t) / (BLOCK_ROWS * HEAD)
    p_scr[...] = (precond_t / jnp.sqrt(mean + 1e-06)).T
    w_out[...] = p_scr[rows_of(block, 64), :].astype(BF16)

    for t in (5, 6):
        sum_copy(t).wait_recv()
    tmp_q[...] += in_q[5].astype(F32) + in_q[6].astype(F32)
    for h in range(HEADS):
        dq_out[:, h * HEAD : (h + 1) * HEAD] = tmp_q[:, h * HEAD : (h + 1) * HEAD].T.astype(BF16)

    wait_recv(zk)
    dk_out[...] = z_total(dk_acc, dk_in, zin_k)

    for one in sent:
        one.wait_send()

    def finish(t, _):
        for one in (ring_copy(qs, "RQ", t), ring_copy(dos, "RD", t), sum_copy(t)):
            one.wait_send()
        return 0

    lax.fori_loop(0, 7, finish, 0)


def per_device(queries, keys, values, saved_out, grad_out, layer_in):
    vmem = pl.BlockSpec(memory_space=pltpu.VMEM)
    hbm = pl.BlockSpec(memory_space=pl.ANY)
    row_chunk = (HEADS, 128, HEAD)
    scratch = [
        pltpu.VMEM((Y,) + row_chunk, BF16),
        pltpu.VMEM((Y,) + row_chunk, BF16),
        pltpu.VMEM(row_chunk, BF16),
        pltpu.VMEM((KEYS, HEAD), BF16),
        pltpu.VMEM((KEYS, HEAD), BF16),
        pltpu.VMEM((HEAD, KEYS), BF16),
        pltpu.VMEM((128, 4096), BF16),
        pltpu.VMEM((Z, 128, 1024), BF16),
        pltpu.VMEM((Z, 128, 1024), BF16),
        pltpu.VMEM((Y, 2, KEYS, 256), F32),
        pltpu.VMEM((Y, 512), F32),
        pltpu.VMEM((16, 512), F32),
        pltpu.VMEM((Y - 1, 16, 512), F32),
        pltpu.VMEM((Y, 512), F32),
        pltpu.VMEM((Y, 512), F32),
        pltpu.VMEM((KEYS, HEAD), F32),
        pltpu.VMEM((KEYS, HEAD), F32),
        pltpu.VMEM((HEAD, 512), F32),
        pltpu.VMEM((7, HEAD, 512), BF16),
        pltpu.VMEM((7, HEAD, 512), BF16),
        pltpu.VMEM((Z, 128, HEAD), F32),
        pltpu.VMEM((Z, 128, HEAD), F32),
        pltpu.VMEM((Z, 128, HEAD), F32),
        pltpu.VMEM((Z, 128, HEAD), F32),
        pltpu.VMEM((3, 128, HEAD), BF16),
        pltpu.VMEM((3, 128, HEAD), BF16),
        pltpu.VMEM((3, 128, HEAD), BF16),
        pltpu.VMEM((3, 128, HEAD), BF16),
        pltpu.VMEM((Z, 128, HEAD), BF16),
        pltpu.VMEM((HEAD, 1024), F32),
        pltpu.VMEM((64, 1024), F32),
        pltpu.VMEM((Y, 64, 128), F32),
        pltpu.VMEM((7, 64, 128), BF16),
        pltpu.VMEM((7, 64, 128), BF16),
        pltpu.VMEM((Z, 64, 128), F32),
        pltpu.VMEM((Z, 64, 128), F32),
        pltpu.VMEM((HEAD, BLOCK_ROWS), F32),
        pltpu.VMEM((BLOCK_ROWS, HEAD), F32),
        pltpu.SemaphoreType.DMA((N_SEMS,)),
        pltpu.SemaphoreType.DMA((N_SEMS,)),
        pltpu.SemaphoreType.DMA((15,)),
    ]
    shapes = (
        jax.ShapeDtypeStruct(queries.shape, BF16),
        jax.ShapeDtypeStruct(keys.shape, BF16),
        jax.ShapeDtypeStruct(values.shape, BF16),
        jax.ShapeDtypeStruct((64, HEAD), BF16),
    )
    return pl.pallas_call(
        kernel,
        out_shape=shapes,
        in_specs=[hbm] * 6,
        out_specs=(vmem,) * 4,
        scratch_shapes=scratch,
        compiler_params=pltpu.CompilerParams(
            collective_id=0, has_side_effects=True, vmem_limit_bytes=60 * 1024 * 1024
        ),
    )(queries, keys, values, saved_out, grad_out, layer_in)


def solution(mesh):
    placed = (P("ctx", "tp"),) * 5 + (P("ctx", None),)
    return jax.shard_map(
        per_device,
        mesh=mesh,
        in_specs=placed,
        out_specs=(P("ctx", "tp"),) * 4,
        check_vma=False,
    )
```

```python
import jax
import jax.numpy as jnp
from jax import lax
from jax.experimental import pallas as pl
from jax.experimental.pallas import tpu as pltpu
from jax.sharding import PartitionSpec as P

HEAD = 128
Y, Z = 8, 4
HEADS = 4
KEYS = 1024
NEWTON = 2
BLOCK_ROWS = 512
FILL = -1e30
SCALE = HEAD ** (-0.5)
SCALE2 = SCALE * 1.4426950408889634
HIGHEST = lax.Precision.HIGHEST
F32 = jnp.float32
BF16 = jnp.bfloat16
NT = (((1,), (1,)), ((), ()))

GROUPS = dict(
    KZ=3, VZ=3, KC=4, VC=4, RQ=8, RD=8, ST=7, DT=7, XZ=2, XR=2, XP=2, DVC=1, ZV=3, VG=3, WC=1, WY=7, WZ=3, GC=1, RS=7, DKC=1, ZK=3
)
BASE, N_SEMS = {}, 0
for _name, _count in GROUPS.items():
    BASE[_name] = N_SEMS
    N_SEMS += _count


def dot(a, b, dims=(((1,), (0,)), ((), ())), precision=None):
    return lax.dot_general(a, b, dims, precision=precision, preferred_element_type=F32)


def dot_high(a, b, dims=(((1,), (0,)), ((), ()))):
    return dot(a, b, dims, precision=HIGHEST)


def kernel(
    q_ref, k_ref, v_ref, o_ref, do_ref, x_ref,
    dq_out, dk_out, dv_out, w_out,
    qs, dos, obuf, kl, vl, kt, xin, xs, xw, passing, ptil,
    tops, stat, stat_in, own_delta, delta_in, factor, delta, dv_acc, dk_acc, tq, out_q, in_q,
    dv_send, dv_in, dk_send, dk_in, zout_v, zin_v, zout_k, zin_k, vg,
    w_full, w_in, wk, wy_out, wy_in, wz_out, wz_in, gbuf, gbuf_in, gt, p_scr,
    send, recv, load,
):
    c = lax.axis_index("ctx")
    core = lax.rem(c, 2)
    z = lax.rem(c // 2, Z)
    y = c // (2 * Z)
    block = z * 2 + core

    def dev(yy, zz, cc):
        return {"ctx": (yy * Z + zz) * 2 + cc}

    sibling = dev(y, z, 1 - core)

    def at_y(step):
        return lax.rem(y + step + Y, Y)

    def at_z(step):
        return lax.rem(z + step, Z)

    def rows_of(number, size):
        return pl.ds(pl.multiple_of(number * size, size), size)

    sent = []

    def copy(src, dst, group, number, device):
        return pltpu.make_async_remote_copy(
            src_ref=src, dst_ref=dst, send_sem=send.at[BASE[group] + number], recv_sem=recv.at[BASE[group] + number],
            device_id=device, device_id_type=pl.DeviceIdType.MESH,
        )

    def start(copies):
        for one in copies:
            one.start()
            sent.append(one)
        return copies

    def wait_recv(copies):
        for one in copies:
            one.wait_recv()

    heads = [pl.ds(h * HEAD, HEAD) for h in range(HEADS)]
    pairs = [(k_ref, kl.at[rows_of(block, 128)])]
    pairs += [(q_ref.at[:, heads[h]], qs.at[y, h]) for h in range(HEADS)]
    pairs += [(do_ref.at[:, heads[h]], dos.at[y, h]) for h in range(HEADS)]
    pairs += [(v_ref, vl.at[rows_of(block, 128)])]
    pairs += [(o_ref.at[:, heads[h]], obuf.at[h]) for h in range(HEADS)]
    pairs += [(x_ref, xin)]
    loads = [pltpu.make_async_copy(src, dst, load.at[n]) for n, (src, dst) in enumerate(pairs)]
    for one in loads:
        one.start()

    barrier = pltpu.get_barrier_semaphore()
    partners = [dev(at_y(i), z, core) for i in range(1, Y)]
    partners += [dev(y, at_z(i), core) for i in range(1, Z)] + [sibling]
    for partner in partners:
        pl.semaphore_signal(barrier, inc=1, device_id=partner, device_id_type=pl.DeviceIdType.MESH)
    for one in loads[:5]:
        one.wait()
    pl.semaphore_wait(barrier, len(partners))

    def ring_target(t):
        return dev(jnp.where(lax.rem(t, 2) == 0, at_y(1), at_y(-1)), z, core)

    def ring_copy(buf, group, t):
        chunk = jnp.where(lax.rem(t, 2) == 0, at_y(-(t // 2)), at_y(t // 2))
        return copy(buf.at[chunk], buf.at[chunk], group, t, ring_target(t))

    def ring_arrival(t):
        return jnp.where(lax.rem(t, 2) == 0, at_y(-1 - t // 2), at_y(1 + t // 2))

    def ring_wait(buf, group, t):
        chunk = ring_arrival(t)
        copy(buf.at[chunk], buf.at[chunk], group, t, sibling).wait_recv()

    def last_copies(buf, group):
        up, down = buf.at[at_y(-3), 0:2], buf.at[at_y(3), 2:4]
        return [copy(up, up, group, 6, ring_target(6)), copy(down, down, group, 7, ring_target(7))]

    def last_wait(buf, group):
        for n in range(2):
            half = buf.at[at_y(4), 2 * n : 2 * n + 2]
            copy(half, half, group, 6 + n, sibling).wait_recv()

    def block_copies(buf, group):
        mine = buf.at[rows_of(block, 128)]
        return [copy(mine, mine, group, i - 1, dev(y, at_z(i), core)) for i in range(1, Z)]

    def core_copy(buf, group, i):
        rows = rows_of(at_z(i) * 2 + core, 128)
        return copy(buf.at[rows], buf.at[rows], group, i, sibling)

    def arrived_block(buf, group, i):
        rows = rows_of(at_z(Z - i) * 2 + core, 128)
        copy(buf.at[rows], buf.at[rows], group, i - 1, sibling).wait_recv()

    def core_wait(buf, group, i):
        rows = rows_of(at_z(i) * 2 + 1 - core, 128)
        copy(buf.at[rows], buf.at[rows], group, i, sibling).wait_recv()

    start(block_copies(kl, "KZ"))
    for t in range(2):
        ring_copy(qs, "RQ", t).start()
    start([core_copy(kl, "KC", 0)])
    for one in loads[5:]:
        one.wait()
    start(block_copies(vl, "VZ"))
    start([core_copy(vl, "VC", 0)])

    stat[...] = jnp.full(stat.shape, FILL, F32)
    tops[...] = jnp.full(tops.shape, FILL, F32)
    dv_acc[...] = jnp.zeros(dv_acc.shape, F32)
    dk_acc[...] = jnp.zeros(dk_acc.shape, F32)
    for h in range(HEADS):
        product = dos[y, h].astype(F32) * obuf[h].astype(F32)
        own_delta[h : h + 1, :] = jnp.sum(product.T, axis=0, keepdims=True)

    def arrange(i, _):
        for zz in range(Z):
            xs[zz, :, rows_of(i, 128)] = xin[:, rows_of(i * Z + zz, 128)]
        return 0

    lax.fori_loop(0, Y, arrange, 0)
    for t in range(2):
        ring_copy(qs, "RQ", t).wait_send()
    for t in range(2):
        ring_copy(dos, "RD", t).start()
    dt = start([copy(own_delta, delta_in.at[i - 1], "DT", i - 1, dev(at_y(i), z, core)) for i in range(1, Y)])

    def row_of(ref, chunk, cols):
        number = lax.broadcasted_iota(jnp.int32, (Y, 256), 0)
        return jnp.sum(jnp.where(number == chunk, ref[0:Y, cols], 0.0), axis=0, keepdims=True)

    def put_row(ref, chunk, cols, row):
        number = lax.broadcasted_iota(jnp.int32, (Y, 256), 0)
        ref[0:Y, cols] = jnp.where(number == chunk, row, ref[0:Y, cols])

    halves = [slice(0, 256), slice(256, 512)]

    def forward(chunk, diagonal):
        for n, cols in enumerate(halves):
            q2 = qs[chunk, 2 * n : 2 * n + 2].reshape(256, HEAD)
            s = dot(kl[...], q2, NT) * SCALE2
            if diagonal:
                key = lax.broadcasted_iota(jnp.int32, (KEYS, 256), 0)
                row = (lax.broadcasted_iota(jnp.int32, (KEYS, 256), 1) & 127) + block * 128
                s = jnp.where(key <= row, s, FILL)
            top = jnp.max(s, axis=0, keepdims=True)
            e = jnp.exp2(s - top)
            ptil[chunk, n] = e
            put_row(tops, chunk, cols, top)
            put_row(stat, chunk, cols, top + jnp.log2(jnp.sum(e, axis=0, keepdims=True)))

    def pass_on(buf, group, t):
        for n in range(2):
            ring_wait(buf, group, t + n)

        onward = [ring_copy(buf, group, t + 2 + n) for n in range(2)] if t < 4 else last_copies(buf, group)
        for one in onward:
            one.start()

    def gather_step(n, _):
        for when, buf, group, t in (
            (0, qs, "RQ", 0), (1, dos, "RD", 0), (3, qs, "RQ", 2), (4, dos, "RD", 2), (5, qs, "RQ", 4), (7, dos, "RD", 4)
        ):
            @pl.when(n == when)
            def _(buf=buf, group=group, t=t):
                pass_on(buf, group, t)

        @pl.when(n == 0)
        def _():
            for i in range(1, Z):
                arrived_block(kl, "KZ", i)
                start([kc[Z - i]])
            for i in range(Z):
                core_wait(kl, "KC", i)
            start(relay)
            forward(y, True)

        @pl.when(n == 2)
        def _():
            start(xz)

        @pl.when(n == 7)
        def _():
            last_wait(qs, "RQ")

        chunk = ring_arrival(jnp.maximum(n - 1, 0))

        @pl.when(jnp.logical_and(n > 0, chunk > y))
        def _():
            forward(chunk, False)

        return 0

    beside = (at_z(1), at_z(3))
    xz = [copy(xs.at[beside[n]], xw.at[z], "XZ", n, dev(y, beside[n], core)) for n in range(2)]
    wide = [pl.ds(0, 512), pl.ds(512, 512)]
    relay = [
        copy(xs.at[at_z(2), :, wide[n]], passing.at[n], "XR", n, dev(y, beside[n], core)) for n in range(2)
    ]
    relay_on = [
        copy(passing.at[n], xw.at[beside[1 - n], :, wide[n]], "XP", n, dev(y, beside[n], core)) for n in range(2)
    ]
    kc = [core_copy(kl, "KC", i) for i in range(Z)]
    xw[z] = xs[z]
    vc = [core_copy(vl, "VC", i) for i in range(Z)]
    lax.fori_loop(0, 8, gather_step, 0)

    st = start([copy(stat, stat_in.at[i - 1], "ST", i - 1, dev(at_y(i), z, core)) for i in range(1, Y)])
    for i in range(1, Z):
        arrived_block(vl, "VZ", i)
        start([vc[Z - i]])
    wait_recv(relay)
    start(relay_on)
    last_wait(dos, "RD")
    kt[...] = kl[...].astype(F32).T.astype(BF16)
    wait_recv(st)
    wait_recv(dt)
    parts = [stat[...]] + [stat_in[i] for i in range(Y - 1)]
    high = parts[0]
    for part in parts[1:]:
        high = jnp.maximum(high, part)
    total = sum(jnp.exp2(part - high) for part in parts)
    factor[...] = jnp.exp2(tops[...] - (high + jnp.log2(total)))
    number = lax.broadcasted_iota(jnp.int32, (Y, 512), 0)
    delta[...] = jnp.zeros(delta.shape, F32)
    for h in range(HEADS):
        cols = slice(h * HEAD, (h + 1) * HEAD)
        part = jnp.where(number[:, cols] == y, own_delta[h : h + 1, :], 0.0)
        for i in range(1, Y):
            part = jnp.where(number[:, cols] == at_y(Y - i), delta_in[i - 1, h : h + 1, :], part)
        delta[:, cols] = part

    def value_tile(chunk):
        for n, cols in enumerate(halves):
            p = (ptil[chunk, n] * row_of(factor, chunk, cols)).astype(BF16)
            dv_acc[...] += dot(p, dos[chunk, 2 * n : 2 * n + 2].reshape(256, HEAD))

    def value_step(n, _):
        chunk = jnp.where(n == 0, y, ring_arrival(jnp.maximum(n - 1, 0)))

        @pl.when(chunk >= y)
        def _():
            value_tile(chunk)

        return 0

    lax.fori_loop(0, 8, value_step, 0)

    def split_cores(acc, out):
        for zz in range(Z):
            out[zz] = acc[rows_of(zz * 2 + 1 - core, 128), :]

    def z_sums(acc, got, out, into, group):
        copies = []
        for i in range(1, Z):
            zz = at_z(i)
            out[i - 1] = (acc[rows_of(zz * 2 + core, 128), :] + got[zz]).astype(BF16)
            copies.append(copy(out.at[i - 1], into.at[i - 1], group, i - 1, dev(y, zz, core)))
        return copies

    def z_total(acc, got, into):
        total = acc[rows_of(block, 128), :] + got[z]
        for i in range(Z - 1):
            total = total + into[i].astype(F32)
        return total.astype(BF16)

    split_cores(dv_acc, dv_send)
    dvc = start([copy(dv_send, dv_in, "DVC", 0, sibling)])

    zv = [copy(zout_v.at[i - 1], zin_v.at[i - 1], "ZV", i - 1, dev(y, at_z(i), core)) for i in range(1, Z)]
    vgc = [copy(vg.at[z], vg.at[z], "VG", i - 1, dev(y, at_z(i), core)) for i in range(1, Z)]
    wc = [copy(w_full.at[rows_of(1 - core, 64)], w_in, "WC", 0, sibling)]
    wy = [copy(wy_out.at[i - 1], wy_in.at[i - 1], "WY", i - 1, dev(at_y(i), z, core)) for i in range(1, Y)]

    wz = [copy(wz_out, wz_in.at[i - 1], "WZ", i - 1, dev(y, at_z(i), core)) for i in range(1, Z)]
    gc = [copy(gbuf, gbuf_in, "GC", 0, sibling)]

    def chain_1():
        wait_recv(dvc)
        z_sums(dv_acc, dv_in, zout_v, zin_v, "ZV")
        start(zv)

    def chain_2():
        wait_recv(zv)
        vg[z] = z_total(dv_acc, dv_in, zin_v)
        start(vgc)
        dv_out[...] = vg[z]

    def chain_3():
        wait_recv(vgc)
        wait_recv(xz + relay_on)
        value_t = vg[...].reshape(512, HEAD).astype(F32).T.astype(BF16)
        for n in range(4):
            cols = slice(n * 256, (n + 1) * 256)
            w_full[:, cols] = dot(value_t, xw[:, :, cols].reshape(512, 256))
        start(wc)

    def chain_4():
        wait_recv(wc)
        kept = w_full[rows_of(core, 64), :] + w_in[...]
        for i in range(Y):
            wk[i] = kept[:, i * 128 : (i + 1) * 128]
        for i in range(1, Y):
            wy_out[i - 1] = wk[at_y(i)].astype(BF16)
        start(wy)

    def chain_5():
        wait_recv(wy)
        g = wk[y]
        for i in range(Y - 1):
            g = g + wy_in[i].astype(F32)
        gbuf[z] = g
        wz_out[...] = g.astype(BF16)
        start(wz)

    def chain_6():
        wait_recv(wz)
        for i in range(1, Z):
            gbuf[at_z(Z - i)] = wz_in[i - 1].astype(F32)
        start(gc)

    def tile(t, chunk):
        for n, cols in enumerate(halves):
            q2 = qs[chunk, 2 * n : 2 * n + 2].reshape(256, HEAD)
            do2 = dos[chunk, 2 * n : 2 * n + 2].reshape(256, HEAD)
            p = ptil[chunk, n] * row_of(factor, chunk, cols)
            dp = dot(vl[...], do2, NT)
            ds = (p * (dp - row_of(delta, chunk, cols)) * SCALE).astype(BF16)
            dk_acc[...] += dot(ds, q2)
            tq[t, :, cols] = dot(kt[...], ds)

    def sum_copy(t):
        return copy(out_q.at[t], in_q.at[t], "RS", t, ring_target(t))

    for i in range(Z):
        core_wait(vl, "VC", i)

    def ring_sum(t):
        total = tq[t]
        if t >= 2:
            sum_copy(t - 2).wait_recv()
            total = total + in_q[t - 2].astype(F32)
        out_q[t] = total.astype(BF16)
        sum_copy(t).start()

    def tile_step(n, _):
        t = jnp.where(n < 2, n, jnp.where(n == 2, 7, n - 1))
        s = t // 2
        chunk = jnp.where(t == 7, y, jnp.where(lax.rem(t, 2) == 0, at_y(4 - s), at_y(s - 3)))

        @pl.when(n == 5)
        def _():
            chain_2()

        @pl.when(chunk >= y)
        def _():
            tile(t, chunk)

        @pl.when(chunk < y)
        def _():
            tq[t] = jnp.zeros((HEAD, 512), F32)

        for when, done in ((0, 0), (1, 1), (3, 2), (4, 3)):
            @pl.when(n == when)
            def _(done=done):
                ring_sum(done)

        @pl.when(n == 0)
        def _():
            chain_1()

        return 0

    lax.fori_loop(0, 8, tile_step, 0)

    split_cores(dk_acc, dk_send)
    dkc = start([copy(dk_send, dk_in, "DKC", 0, sibling)])
    ring_sum(4)
    ring_sum(5)
    chain_3()
    wait_recv(dkc)
    zk = start(z_sums(dk_acc, dk_in, zout_k, zin_k, "ZK"))
    chain_4()
    ring_sum(6)
    chain_5()
    for t in (5, 6):
        sum_copy(t).wait_recv()
    for h in range(HEADS):
        cols = slice(h * HEAD, (h + 1) * HEAD)
        total = tq[7, :, cols] + in_q[5, :, cols].astype(F32) + in_q[6, :, cols].astype(F32)
        dq_out[:, cols] = total.T.astype(BF16)
    wait_recv(zk)
    dk_out[...] = z_total(dk_acc, dk_in, zin_k)
    chain_6()

    wait_recv(gc)
    for zz in range(Z):
        gt[rows_of(core, 64), zz * 128 : (zz + 1) * 128] = gbuf[zz]
        gt[rows_of(1 - core, 64), zz * 128 : (zz + 1) * 128] = gbuf_in[zz]

    grad_t = gt[...]
    gram = dot_high(grad_t, grad_t, NT)
    eye = (
        lax.broadcasted_iota(jnp.int32, (HEAD, HEAD), 0) == lax.broadcasted_iota(jnp.int32, (HEAD, HEAD), 1)
    ).astype(F32)

    def all_sum(a):
        return jnp.sum(jnp.sum(a, axis=0, keepdims=True), axis=1, keepdims=True)

    squares = all_sum(gram * eye)
    gram_squares = all_sum(gram * gram)

    def inverse_root(size):
        shift = 0.1 * squares / size + 1e-06
        norm = jnp.sqrt(gram_squares + 2.0 * shift * squares + size * shift * shift)
        matrix = (gram + shift * eye) / norm
        root = None
        for iteration in range(NEWTON):
            part = (5.0 * eye - matrix) * 0.25
            root = part if root is None else dot_high(root, part)
            if iteration < NEWTON - 1:
                square = dot_high(part, part)
                matrix = dot_high(dot_high(square, square), matrix)
        return root

    mixed = dot_high(inverse_root(BLOCK_ROWS), inverse_root(HEAD))
    precond_t = dot_high(mixed, grad_t)
    mean = all_sum(precond_t * precond_t) / (BLOCK_ROWS * HEAD)
    p_scr[...] = (precond_t / jnp.sqrt(mean + 1e-06)).T
    w_out[...] = p_scr[rows_of(block, 64), :].astype(BF16)

    for one in sent:
        one.wait_send()

    for one in last_copies(qs, "RQ") + last_copies(dos, "RD") + [sum_copy(6)]:
        one.wait_send()

    for t in range(2, 6):
        ring_copy(qs, "RQ", t).wait_send()
    for t in range(6):
        ring_copy(dos, "RD", t).wait_send()
        sum_copy(t).wait_send()


def per_device(queries, keys, values, saved_out, grad_out, layer_in):
    vmem = pl.BlockSpec(memory_space=pltpu.VMEM)
    hbm = pl.BlockSpec(memory_space=pl.ANY)
    row_chunk = (HEADS, 128, HEAD)
    scratch = [
        pltpu.VMEM((Y,) + row_chunk, BF16),
        pltpu.VMEM((Y,) + row_chunk, BF16),
        pltpu.VMEM(row_chunk, BF16),
        pltpu.VMEM((KEYS, HEAD), BF16),
        pltpu.VMEM((KEYS, HEAD), BF16),
        pltpu.VMEM((HEAD, KEYS), BF16),
        pltpu.VMEM((128, 4096), BF16),
        pltpu.VMEM((Z, 128, 1024), BF16),
        pltpu.VMEM((Z, 128, 1024), BF16),
        pltpu.VMEM((2, 128, 512), BF16),
        pltpu.VMEM((Y, 2, KEYS, 256), F32),
        pltpu.VMEM((Y, 512), F32),
        pltpu.VMEM((Y, 512), F32),
        pltpu.VMEM((Y - 1, Y, 512), F32),
        pltpu.VMEM((8, HEAD), F32),
        pltpu.VMEM((Y - 1, 8, HEAD), F32),
        pltpu.VMEM((Y, 512), F32),
        pltpu.VMEM((Y, 512), F32),
        pltpu.VMEM((KEYS, HEAD), F32),
        pltpu.VMEM((KEYS, HEAD), F32),
        pltpu.VMEM((8, HEAD, 512), F32),
        pltpu.VMEM((7, HEAD, 512), BF16),
        pltpu.VMEM((7, HEAD, 512), BF16),
        pltpu.VMEM((Z, 128, HEAD), F32),
        pltpu.VMEM((Z, 128, HEAD), F32),
        pltpu.VMEM((Z, 128, HEAD), F32),
        pltpu.VMEM((Z, 128, HEAD), F32),
        pltpu.VMEM((3, 128, HEAD), BF16),
        pltpu.VMEM((3, 128, HEAD), BF16),
        pltpu.VMEM((3, 128, HEAD), BF16),
        pltpu.VMEM((3, 128, HEAD), BF16),
        pltpu.VMEM((Z, 128, HEAD), BF16),
        pltpu.VMEM((HEAD, 1024), F32),
        pltpu.VMEM((64, 1024), F32),
        pltpu.VMEM((Y, 64, 128), F32),
        pltpu.VMEM((7, 64, 128), BF16),
        pltpu.VMEM((7, 64, 128), BF16),
        pltpu.VMEM((64, 128), BF16),
        pltpu.VMEM((3, 64, 128), BF16),
        pltpu.VMEM((Z, 64, 128), F32),
        pltpu.VMEM((Z, 64, 128), F32),
        pltpu.VMEM((HEAD, BLOCK_ROWS), F32),
        pltpu.VMEM((BLOCK_ROWS, HEAD), F32),
        pltpu.SemaphoreType.DMA((N_SEMS,)),
        pltpu.SemaphoreType.DMA((N_SEMS,)),
        pltpu.SemaphoreType.DMA((15,)),
    ]
    shapes = (
        jax.ShapeDtypeStruct(queries.shape, BF16),
        jax.ShapeDtypeStruct(keys.shape, BF16),
        jax.ShapeDtypeStruct(values.shape, BF16),
        jax.ShapeDtypeStruct((64, HEAD), BF16),
    )
    return pl.pallas_call(
        kernel,
        out_shape=shapes,
        in_specs=[hbm] * 6,
        out_specs=(vmem,) * 4,
        scratch_shapes=scratch,
        compiler_params=pltpu.CompilerParams(
            collective_id=0, has_side_effects=True, vmem_limit_bytes=60 * 1024 * 1024
        ),
    )(queries, keys, values, saved_out, grad_out, layer_in)


def solution(mesh):
    placed = (P("ctx", "tp"),) * 5 + (P("ctx", None),)
    return jax.shard_map(
        per_device,
        mesh=mesh,
        in_specs=placed,
        out_specs=(P("ctx", "tp"),) * 4,
        check_vma=False,
    )
```

```python
import jax
import jax.numpy as jnp
from jax import lax
from jax.experimental import pallas as pl
from jax.experimental.pallas import tpu as pltpu
from jax.sharding import PartitionSpec as P

HEAD = 128
Y, Z = 8, 4
HEADS = 4
KEYS = 1024
NEWTON = 2
BLOCK_ROWS = 512
FILL = -1e30
SCALE = HEAD ** (-0.5)
SCALE2 = SCALE * 1.4426950408889634
HIGHEST = lax.Precision.HIGHEST
F32 = jnp.float32
BF16 = jnp.bfloat16
NT = (((1,), (1,)), ((), ()))

GROUPS = dict(
    KZ=3, VZ=3, KC=4, VC=4, RQ=8, RD=8, ST=7, DT=7, XZ=2, XR=2, XP=2, DVC=1, ZV=3, VG=3, WC=1, WY=7, WZ=3, GC=1, RS=7, DKC=1, ZK=3
)
BASE, N_SEMS = {}, 0
for _name, _count in GROUPS.items():
    BASE[_name] = N_SEMS
    N_SEMS += _count


def dot(a, b, dims=(((1,), (0,)), ((), ())), precision=None):
    return lax.dot_general(a, b, dims, precision=precision, preferred_element_type=F32)


def dot_high(a, b, dims=(((1,), (0,)), ((), ()))):
    return dot(a, b, dims, precision=HIGHEST)


def kernel(
    q_ref, k_ref, v_ref, o_ref, do_ref, x_ref,
    dq_out, dk_out, dv_out, w_out,
    qs, dos, obuf, kl, vl, kt, xin, xs, xw, passing, ptil,
    tops, stat, stat_in, own_delta, delta_in, factor, delta, dv_acc, dk_acc, tq, out_q, in_q,
    dv_send, dv_in, dk_send, dk_in, zout_v, zin_v, zout_k, zin_k, vg,
    w_full, w_in, wk, wy_out, wy_in, wz_out, wz_in, gbuf, gbuf_in, gt, p_scr,
    send, recv, load,
):
    c = lax.axis_index("ctx")
    core = lax.rem(c, 2)
    z = lax.rem(c // 2, Z)
    y = c // (2 * Z)
    block = z * 2 + core

    def dev(yy, zz, cc):
        return {"ctx": (yy * Z + zz) * 2 + cc}

    sibling = dev(y, z, 1 - core)

    def at_y(step):
        return lax.rem(y + step + Y, Y)

    def at_z(step):
        return lax.rem(z + step, Z)

    def rows_of(number, size):
        return pl.ds(pl.multiple_of(number * size, size), size)

    sent = []

    def copy(src, dst, group, number, device):
        return pltpu.make_async_remote_copy(
            src_ref=src, dst_ref=dst, send_sem=send.at[BASE[group] + number], recv_sem=recv.at[BASE[group] + number],
            device_id=device, device_id_type=pl.DeviceIdType.MESH,
        )

    def start(copies):
        for one in copies:
            one.start()
            sent.append(one)
        return copies

    def wait_recv(copies):
        for one in copies:
            one.wait_recv()

    heads = [pl.ds(h * HEAD, HEAD) for h in range(HEADS)]
    pairs = [(k_ref, kl.at[rows_of(block, 128)])]
    pairs += [(q_ref.at[:, heads[h]], qs.at[y, h]) for h in range(HEADS)]
    pairs += [(do_ref.at[:, heads[h]], dos.at[y, h]) for h in range(HEADS)]
    pairs += [(v_ref, vl.at[rows_of(block, 128)])]
    pairs += [(o_ref.at[:, heads[h]], obuf.at[h]) for h in range(HEADS)]
    pairs += [(x_ref, xin)]
    loads = [pltpu.make_async_copy(src, dst, load.at[n]) for n, (src, dst) in enumerate(pairs)]
    for one in loads:
        one.start()

    barrier = pltpu.get_barrier_semaphore()
    partners = [dev(at_y(i), z, core) for i in range(1, Y)]
    partners += [dev(y, at_z(i), core) for i in range(1, Z)] + [sibling]
    for partner in partners:
        pl.semaphore_signal(barrier, inc=1, device_id=partner, device_id_type=pl.DeviceIdType.MESH)
    for one in loads[:5]:
        one.wait()
    pl.semaphore_wait(barrier, len(partners))

    def ring_target(t):
        return dev(jnp.where(lax.rem(t, 2) == 0, at_y(1), at_y(-1)), z, core)

    def ring_copy(buf, group, t):
        chunk = jnp.where(lax.rem(t, 2) == 0, at_y(-(t // 2)), at_y(t // 2))
        return copy(buf.at[chunk], buf.at[chunk], group, t, ring_target(t))

    def ring_arrival(t):
        return jnp.where(lax.rem(t, 2) == 0, at_y(-1 - t // 2), at_y(1 + t // 2))

    def ring_wait(buf, group, t):
        chunk = ring_arrival(t)
        copy(buf.at[chunk], buf.at[chunk], group, t, sibling).wait_recv()

    def last_copies(buf, group):
        up, down = buf.at[at_y(-3), 0:2], buf.at[at_y(3), 2:4]
        return [copy(up, up, group, 6, ring_target(6)), copy(down, down, group, 7, ring_target(7))]

    def last_wait(buf, group):
        for n in range(2):
            half = buf.at[at_y(4), 2 * n : 2 * n + 2]
            copy(half, half, group, 6 + n, sibling).wait_recv()

    def block_copies(buf, group):
        mine = buf.at[rows_of(block, 128)]
        return [copy(mine, mine, group, i - 1, dev(y, at_z(i), core)) for i in range(1, Z)]

    def core_copy(buf, group, i):
        rows = rows_of(at_z(i) * 2 + core, 128)
        return copy(buf.at[rows], buf.at[rows], group, i, sibling)

    def arrived_block(buf, group, i):
        rows = rows_of(at_z(Z - i) * 2 + core, 128)
        copy(buf.at[rows], buf.at[rows], group, i - 1, sibling).wait_recv()

    def core_wait(buf, group, i):
        rows = rows_of(at_z(i) * 2 + 1 - core, 128)
        copy(buf.at[rows], buf.at[rows], group, i, sibling).wait_recv()

    start(block_copies(kl, "KZ"))
    for t in range(2):
        ring_copy(qs, "RQ", t).start()
    start([core_copy(kl, "KC", 0)])
    for one in loads[5:]:
        one.wait()
    start(block_copies(vl, "VZ"))
    start([core_copy(vl, "VC", 0)])

    stat[...] = jnp.full(stat.shape, FILL, F32)
    tops[...] = jnp.full(tops.shape, FILL, F32)
    dv_acc[...] = jnp.zeros(dv_acc.shape, F32)
    dk_acc[...] = jnp.zeros(dk_acc.shape, F32)
    for h in range(HEADS):
        product = dos[y, h].astype(F32) * obuf[h].astype(F32)
        own_delta[h : h + 1, :] = jnp.sum(product.T, axis=0, keepdims=True)

    def arrange(i, _):
        for zz in range(Z):
            xs[zz, :, rows_of(i, 128)] = xin[:, rows_of(i * Z + zz, 128)]
        return 0

    lax.fori_loop(0, Y, arrange, 0)
    for t in range(2):
        ring_copy(dos, "RD", t).start()
    dt = start([copy(own_delta, delta_in.at[i - 1], "DT", i - 1, dev(at_y(i), z, core)) for i in range(1, Y)])

    def row_of(ref, chunk, cols):
        number = lax.broadcasted_iota(jnp.int32, (Y, 256), 0)
        return jnp.sum(jnp.where(number == chunk, ref[0:Y, cols], 0.0), axis=0, keepdims=True)

    def put_row(ref, chunk, cols, row):
        number = lax.broadcasted_iota(jnp.int32, (Y, 256), 0)
        ref[0:Y, cols] = jnp.where(number == chunk, row, ref[0:Y, cols])

    halves = [slice(0, 256), slice(256, 512)]

    def forward(chunk, diagonal):
        for n, cols in enumerate(halves):
            q2 = qs[chunk, 2 * n : 2 * n + 2].reshape(256, HEAD)
            s = dot(kl[...], q2, NT) * SCALE2
            if diagonal:
                key = lax.broadcasted_iota(jnp.int32, (KEYS, 256), 0)
                row = (lax.broadcasted_iota(jnp.int32, (KEYS, 256), 1) & 127) + block * 128
                s = jnp.where(key <= row, s, FILL)
            top = jnp.max(s, axis=0, keepdims=True)
            e = jnp.exp2(s - top)
            ptil[chunk, n] = e
            put_row(tops, chunk, cols, top)
            put_row(stat, chunk, cols, top + jnp.log2(jnp.sum(e, axis=0, keepdims=True)))

    def pass_on(buf, group, t):
        for n in range(2):
            ring_wait(buf, group, t + n)

        onward = [ring_copy(buf, group, t + 2 + n) for n in range(2)] if t < 4 else last_copies(buf, group)
        for one in onward:
            one.start()

    def gather_step(n, _):
        for when, buf, group, t in (
            (0, qs, "RQ", 0), (1, dos, "RD", 0), (3, qs, "RQ", 2), (4, dos, "RD", 2), (5, qs, "RQ", 4), (7, dos, "RD", 4)
        ):
            @pl.when(n == when)
            def _(buf=buf, group=group, t=t):
                pass_on(buf, group, t)

        @pl.when(n == 0)
        def _():
            for i in range(1, Z):
                arrived_block(kl, "KZ", i)
                start([kc[Z - i]])
            for i in range(Z):
                core_wait(kl, "KC", i)
            start(relay)
            forward(y, True)

        @pl.when(n == 2)
        def _():
            start(xz)

        @pl.when(n == 7)
        def _():
            last_wait(qs, "RQ")

        chunk = ring_arrival(jnp.maximum(n - 1, 0))

        @pl.when(jnp.logical_and(n > 0, chunk > y))
        def _():
            forward(chunk, False)

        return 0

    beside = (at_z(1), at_z(3))
    xz = [copy(xs.at[beside[n]], xw.at[z], "XZ", n, dev(y, beside[n], core)) for n in range(2)]
    wide = [pl.ds(0, 512), pl.ds(512, 512)]
    relay = [
        copy(xs.at[at_z(2), :, wide[n]], passing.at[n], "XR", n, dev(y, beside[n], core)) for n in range(2)
    ]
    relay_on = [
        copy(passing.at[n], xw.at[beside[1 - n], :, wide[n]], "XP", n, dev(y, beside[n], core)) for n in range(2)
    ]
    kc = [core_copy(kl, "KC", i) for i in range(Z)]
    xw[z] = xs[z]
    vc = [core_copy(vl, "VC", i) for i in range(Z)]
    lax.fori_loop(0, 8, gather_step, 0)

    st = start([copy(stat, stat_in.at[i - 1], "ST", i - 1, dev(at_y(i), z, core)) for i in range(1, Y)])
    for i in range(1, Z):
        arrived_block(vl, "VZ", i)
        start([vc[Z - i]])
    wait_recv(relay)
    start(relay_on)
    last_wait(dos, "RD")
    kt[...] = kl[...].astype(F32).T.astype(BF16)
    wait_recv(st)
    wait_recv(dt)
    parts = [stat[...]] + [stat_in[i] for i in range(Y - 1)]
    high = parts[0]
    for part in parts[1:]:
        high = jnp.maximum(high, part)
    total = sum(jnp.exp2(part - high) for part in parts)
    factor[...] = jnp.exp2(tops[...] - (high + jnp.log2(total)))
    number = lax.broadcasted_iota(jnp.int32, (Y, 512), 0)
    delta[...] = jnp.zeros(delta.shape, F32)
    for h in range(HEADS):
        cols = slice(h * HEAD, (h + 1) * HEAD)
        part = jnp.where(number[:, cols] == y, own_delta[h : h + 1, :], 0.0)
        for i in range(1, Y):
            part = jnp.where(number[:, cols] == at_y(Y - i), delta_in[i - 1, h : h + 1, :], part)
        delta[:, cols] = part

    def value_tile(chunk):
        for n, cols in enumerate(halves):
            p = (ptil[chunk, n] * row_of(factor, chunk, cols)).astype(BF16)
            dv_acc[...] += dot(p, dos[chunk, 2 * n : 2 * n + 2].reshape(256, HEAD))

    def value_step(n, _):
        chunk = jnp.where(n == 0, y, ring_arrival(jnp.maximum(n - 1, 0)))

        @pl.when(chunk >= y)
        def _():
            value_tile(chunk)

        return 0

    lax.fori_loop(0, 8, value_step, 0)

    def split_cores(acc, out):
        for zz in range(Z):
            out[zz] = acc[rows_of(zz * 2 + 1 - core, 128), :]

    def z_sums(acc, got, out, into, group):
        copies = []
        for i in range(1, Z):
            zz = at_z(i)
            out[i - 1] = (acc[rows_of(zz * 2 + core, 128), :] + got[zz]).astype(BF16)
            copies.append(copy(out.at[i - 1], into.at[i - 1], group, i - 1, dev(y, zz, core)))
        return copies

    def z_total(acc, got, into):
        total = acc[rows_of(block, 128), :] + got[z]
        for i in range(Z - 1):
            total = total + into[i].astype(F32)
        return total.astype(BF16)

    split_cores(dv_acc, dv_send)
    dvc = start([copy(dv_send, dv_in, "DVC", 0, sibling)])

    zv = [copy(zout_v.at[i - 1], zin_v.at[i - 1], "ZV", i - 1, dev(y, at_z(i), core)) for i in range(1, Z)]
    vgc = [copy(vg.at[z], vg.at[z], "VG", i - 1, dev(y, at_z(i), core)) for i in range(1, Z)]
    wc = [copy(w_full.at[rows_of(1 - core, 64)], w_in, "WC", 0, sibling)]
    wy = [copy(wy_out.at[i - 1], wy_in.at[i - 1], "WY", i - 1, dev(at_y(i), z, core)) for i in range(1, Y)]

    wz = [copy(wz_out, wz_in.at[i - 1], "WZ", i - 1, dev(y, at_z(i), core)) for i in range(1, Z)]
    gc = [copy(gbuf, gbuf_in, "GC", 0, sibling)]

    def chain_1():
        wait_recv(dvc)
        z_sums(dv_acc, dv_in, zout_v, zin_v, "ZV")
        start(zv)

    def chain_2():
        wait_recv(zv)
        vg[z] = z_total(dv_acc, dv_in, zin_v)
        start(vgc)
        dv_out[...] = vg[z]

    def chain_3():
        wait_recv(vgc)
        wait_recv(xz + relay_on)
        value_t = vg[...].reshape(512, HEAD).astype(F32).T.astype(BF16)
        for n in range(4):
            cols = slice(n * 256, (n + 1) * 256)
            w_full[:, cols] = dot(value_t, xw[:, :, cols].reshape(512, 256))
        start(wc)

    def chain_4():
        wait_recv(wc)
        kept = w_full[rows_of(core, 64), :] + w_in[...]
        for i in range(Y):
            wk[i] = kept[:, i * 128 : (i + 1) * 128]
        for i in range(1, Y):
            wy_out[i - 1] = wk[at_y(i)].astype(BF16)
        start(wy)

    def chain_5():
        wait_recv(wy)
        g = wk[y]
        for i in range(Y - 1):
            g = g + wy_in[i].astype(F32)
        gbuf[z] = g
        wz_out[...] = g.astype(BF16)
        start(wz)

    def chain_6():
        wait_recv(wz)
        for i in range(1, Z):
            gbuf[at_z(Z - i)] = wz_in[i - 1].astype(F32)
        start(gc)

    def tile(t, chunk):
        for n, cols in enumerate(halves):
            q2 = qs[chunk, 2 * n : 2 * n + 2].reshape(256, HEAD)
            do2 = dos[chunk, 2 * n : 2 * n + 2].reshape(256, HEAD)
            p = ptil[chunk, n] * row_of(factor, chunk, cols)
            dp = dot(vl[...], do2, NT)
            ds = (p * (dp - row_of(delta, chunk, cols)) * SCALE).astype(BF16)
            dk_acc[...] += dot(ds, q2)
            tq[t, :, cols] = dot(kt[...], ds)

    def sum_copy(t):
        return copy(out_q.at[t], in_q.at[t], "RS", t, ring_target(t))

    for i in range(Z):
        core_wait(vl, "VC", i)

    def ring_sum(t):
        total = tq[t]
        if t >= 2:
            sum_copy(t - 2).wait_recv()
            total = total + in_q[t - 2].astype(F32)
        out_q[t] = total.astype(BF16)
        sum_copy(t).start()

    def tile_step(n, _):
        t = jnp.where(n < 2, n, jnp.where(n == 2, 7, n - 1))
        s = t // 2
        chunk = jnp.where(t == 7, y, jnp.where(lax.rem(t, 2) == 0, at_y(4 - s), at_y(s - 3)))

        @pl.when(n == 5)
        def _():
            chain_2()

        @pl.when(chunk >= y)
        def _():
            tile(t, chunk)

        @pl.when(chunk < y)
        def _():
            tq[t] = jnp.zeros((HEAD, 512), F32)

        for when, done in ((0, 0), (1, 1), (3, 2), (4, 3)):
            @pl.when(n == when)
            def _(done=done):
                ring_sum(done)

        @pl.when(n == 0)
        def _():
            chain_1()

        return 0

    lax.fori_loop(0, 8, tile_step, 0)

    split_cores(dk_acc, dk_send)
    dkc = start([copy(dk_send, dk_in, "DKC", 0, sibling)])
    ring_sum(4)
    ring_sum(5)
    chain_3()
    wait_recv(dkc)
    zk = start(z_sums(dk_acc, dk_in, zout_k, zin_k, "ZK"))
    chain_4()
    ring_sum(6)
    chain_5()
    for t in (5, 6):
        sum_copy(t).wait_recv()
    for h in range(HEADS):
        cols = slice(h * HEAD, (h + 1) * HEAD)
        total = tq[7, :, cols] + in_q[5, :, cols].astype(F32) + in_q[6, :, cols].astype(F32)
        dq_out[:, cols] = total.T.astype(BF16)
    wait_recv(zk)
    dk_out[...] = z_total(dk_acc, dk_in, zin_k)
    chain_6()

    wait_recv(gc)
    for zz in range(Z):
        gt[rows_of(core, 64), zz * 128 : (zz + 1) * 128] = gbuf[zz]
        gt[rows_of(1 - core, 64), zz * 128 : (zz + 1) * 128] = gbuf_in[zz]

    grad_t = gt[...]
    gram = dot_high(grad_t, grad_t, NT)
    eye = (
        lax.broadcasted_iota(jnp.int32, (HEAD, HEAD), 0) == lax.broadcasted_iota(jnp.int32, (HEAD, HEAD), 1)
    ).astype(F32)

    def all_sum(a):
        return jnp.sum(jnp.sum(a, axis=0, keepdims=True), axis=1, keepdims=True)

    squares = all_sum(gram * eye)
    gram_squares = all_sum(gram * gram)

    def inverse_root(size):
        shift = 0.1 * squares / size + 1e-06
        norm = jnp.sqrt(gram_squares + 2.0 * shift * squares + size * shift * shift)
        matrix = (gram + shift * eye) / norm
        root = None
        for iteration in range(NEWTON):
            part = (5.0 * eye - matrix) * 0.25
            root = part if root is None else dot_high(root, part)
            if iteration < NEWTON - 1:
                square = dot_high(part, part)
                matrix = dot_high(dot_high(square, square), matrix)
        return root

    mixed = dot_high(inverse_root(BLOCK_ROWS), inverse_root(HEAD))
    precond_t = dot_high(mixed, grad_t)
    mean = all_sum(precond_t * precond_t) / (BLOCK_ROWS * HEAD)
    p_scr[...] = (precond_t / jnp.sqrt(mean + 1e-06)).T
    w_out[...] = p_scr[rows_of(block, 64), :].astype(BF16)

    for one in sent:
        one.wait_send()

    for one in last_copies(qs, "RQ") + last_copies(dos, "RD") + [sum_copy(6)]:
        one.wait_send()

    for t in range(6):
        ring_copy(qs, "RQ", t).wait_send()
    for t in range(6):
        ring_copy(dos, "RD", t).wait_send()
        sum_copy(t).wait_send()


def per_device(queries, keys, values, saved_out, grad_out, layer_in):
    vmem = pl.BlockSpec(memory_space=pltpu.VMEM)
    hbm = pl.BlockSpec(memory_space=pl.ANY)
    row_chunk = (HEADS, 128, HEAD)
    scratch = [
        pltpu.VMEM((Y,) + row_chunk, BF16),
        pltpu.VMEM((Y,) + row_chunk, BF16),
        pltpu.VMEM(row_chunk, BF16),
        pltpu.VMEM((KEYS, HEAD), BF16),
        pltpu.VMEM((KEYS, HEAD), BF16),
        pltpu.VMEM((HEAD, KEYS), BF16),
        pltpu.VMEM((128, 4096), BF16),
        pltpu.VMEM((Z, 128, 1024), BF16),
        pltpu.VMEM((Z, 128, 1024), BF16),
        pltpu.VMEM((2, 128, 512), BF16),
        pltpu.VMEM((Y, 2, KEYS, 256), F32),
        pltpu.VMEM((Y, 512), F32),
        pltpu.VMEM((Y, 512), F32),
        pltpu.VMEM((Y - 1, Y, 512), F32),
        pltpu.VMEM((8, HEAD), F32),
        pltpu.VMEM((Y - 1, 8, HEAD), F32),
        pltpu.VMEM((Y, 512), F32),
        pltpu.VMEM((Y, 512), F32),
        pltpu.VMEM((KEYS, HEAD), F32),
        pltpu.VMEM((KEYS, HEAD), F32),
        pltpu.VMEM((8, HEAD, 512), F32),
        pltpu.VMEM((7, HEAD, 512), BF16),
        pltpu.VMEM((7, HEAD, 512), BF16),
        pltpu.VMEM((Z, 128, HEAD), F32),
        pltpu.VMEM((Z, 128, HEAD), F32),
        pltpu.VMEM((Z, 128, HEAD), F32),
        pltpu.VMEM((Z, 128, HEAD), F32),
        pltpu.VMEM((3, 128, HEAD), BF16),
        pltpu.VMEM((3, 128, HEAD), BF16),
        pltpu.VMEM((3, 128, HEAD), BF16),
        pltpu.VMEM((3, 128, HEAD), BF16),
        pltpu.VMEM((Z, 128, HEAD), BF16),
        pltpu.VMEM((HEAD, 1024), F32),
        pltpu.VMEM((64, 1024), F32),
        pltpu.VMEM((Y, 64, 128), F32),
        pltpu.VMEM((7, 64, 128), BF16),
        pltpu.VMEM((7, 64, 128), BF16),
        pltpu.VMEM((64, 128), BF16),
        pltpu.VMEM((3, 64, 128), BF16),
        pltpu.VMEM((Z, 64, 128), F32),
        pltpu.VMEM((Z, 64, 128), F32),
        pltpu.VMEM((HEAD, BLOCK_ROWS), F32),
        pltpu.VMEM((BLOCK_ROWS, HEAD), F32),
        pltpu.SemaphoreType.DMA((N_SEMS,)),
        pltpu.SemaphoreType.DMA((N_SEMS,)),
        pltpu.SemaphoreType.DMA((15,)),
    ]
    shapes = (
        jax.ShapeDtypeStruct(queries.shape, BF16),
        jax.ShapeDtypeStruct(keys.shape, BF16),
        jax.ShapeDtypeStruct(values.shape, BF16),
        jax.ShapeDtypeStruct((64, HEAD), BF16),
    )
    return pl.pallas_call(
        kernel,
        out_shape=shapes,
        in_specs=[hbm] * 6,
        out_specs=(vmem,) * 4,
        scratch_shapes=scratch,
        compiler_params=pltpu.CompilerParams(
            collective_id=0, has_side_effects=True, vmem_limit_bytes=60 * 1024 * 1024
        ),
    )(queries, keys, values, saved_out, grad_out, layer_in)


def solution(mesh):
    placed = (P("ctx", "tp"),) * 5 + (P("ctx", None),)
    return jax.shard_map(
        per_device,
        mesh=mesh,
        in_specs=placed,
        out_specs=(P("ctx", "tp"),) * 4,
        check_vma=False,
    )
```
